256 devices in a mesh: leaf: 64 (over z, x, core), near: 4 (over y).
Axes of the slice: x: 4, y: 4, z: 8, core: 2. Of those that a mesh axis runs over, the one named last changes fastest.
Arguments:
- vectors: bfloat16 [256, 131072], P(None, 'leaf'), may hold values from -6 to 6
- near_blocks: bfloat16 [512, 32, 256, 256], P('leaf', 'near'), may hold values from -0.0625 to 0.0625
- near_cols: int32 [512, 32], P('leaf', 'near'), may hold values from 0 to 511, as said below
- near_count: int32 [512], P('leaf'), may hold values from 8 to 32, as said below
- col_basis: bfloat16 [64, 131072], P(None, 'leaf'), may hold values from -0.375 to 0.375
- row_basis: bfloat16 [64, 131072], P(None, 'leaf'), may hold values from -0.1875 to 0.1875
- local_transfer: bfloat16 [448, 64, 128], P('leaf'), may hold values from -0.5 to 0.5
- local_coupling: bfloat16 [960, 64, 512], P('leaf', None, 'near'), may hold values from -0.25 to 0.25
- local_partners: int32 [960, 8], P('leaf', 'near'), may hold values from 0 to 511, as said below
- upper_transfer: bfloat16 [63, 64, 128], replicated, may hold values from -0.5 to 0.5
- upper_coupling: bfloat16 [63, 64, 512], P(None, None, 'near'), may hold values from -0.25 to 0.25
- upper_partners: int32 [63, 8], P(None, 'near'), may hold values from 0 to 31
Outputs:
- result: bfloat16 [256, 131072], P('near', 'leaf')
The draws below stay inside these ranges and needn't reach their ends.
Inputs may be any that keep to these rules, and one draw needn't show every extreme that they name: `near_cols`: slot 0 of every leaf row names that leaf; every entry names a leaf at most 8 away. `near_count`: some leaf row has all 32 slots live. `local_partners`: a node of level k names nodes of level k at most 8 / 2**k away.
All inputs are finite; a program needn't handle non-finite values.
Results may differ from the reference program's by a relative error of at most 0.004.
Values may be sent and summed in bfloat16 or wider, within the bound.
A program may use at most 128 MiB of HBM per device.

```python
import jax
import jax.numpy as jnp
from jax import lax

LEAF = 256
RANK = 64
COLS = 256
NEAR = 32
FAR = 8
LEAF_DEV = 8
LEAVES = 512
ROWS = 131072
LOCAL_NODES = 960
LOCAL_PARENTS = 448
UPPER = 63
N_LEAF = 64


def draw_near_cols(key, part):
    key = jax.random.fold_in(key, 11)
    steps = jax.random.randint(key, (LEAVES, NEAR), -LEAF_DEV, LEAF_DEV + 1)
    own = jnp.arange(LEAVES, dtype=jnp.int32)[:, None]
    picks = jnp.clip(own + steps, 0, LEAVES - 1)
    picks = jnp.concatenate([own, picks[:, 1:]], axis=1)
    return picks.astype(jnp.int32)


def draw_near_count(key, part):
    key = jax.random.fold_in(key, 12)
    first, second = jax.random.split(key)
    counts = jax.random.randint(first, (LEAVES,), NEAR // 4, NEAR + 1)
    fullest = jax.random.randint(second, (), 0, LEAVES)
    marks = jnp.arange(LEAVES, dtype=jnp.int32) == fullest
    return jnp.where(marks, NEAR, counts).astype(jnp.int32)


def draw_local_partners(key, part):
    key = jax.random.fold_in(key, 13)
    devices = UPPER + 1
    pieces = []
    for level in range(LEAF_DEV.bit_length()):
        count = LEAF_DEV >> level
        total = devices * count
        own = jnp.arange(total, dtype=jnp.int32).reshape(devices, count, 1)
        steps = jax.random.randint(jax.random.fold_in(key, level), (devices, count, FAR), -count, count + 1)
        pieces.append(jnp.clip(own + steps, 0, total - 1))
    joined = jnp.concatenate(pieces, axis=1)
    return joined.reshape(devices * (2 * LEAF_DEV - 1), FAR).astype(jnp.int32)


def draw_upper_partners(key, part):
    key = jax.random.fold_in(key, 14)
    pieces = []
    for level in range((UPPER + 1).bit_length() - 1):
        count = UPPER + 1 >> level + 1
        pieces.append(jax.random.randint(jax.random.fold_in(key, level), (count, FAR), 0, count))
    return jnp.concatenate(pieces, axis=0).astype(jnp.int32)


def level_of(own_key, extent, shards, low, largest):
    gain, own = 1.0, jax.random.fold_in(own_key, 6)
    for dim, shards_of in shards:
        draws = jnp.exp(jax.random.uniform(jax.random.fold_in(own, dim), (shards_of,), jnp.float32, low / len(shards), largest / len(shards)))
        gain = gain * jnp.repeat(draws, extent[dim] // shards_of).reshape([-1 if axis == dim else 1 for axis in range(len(extent))])
    return gain


def centred(rng, extent, deviation, reach, cuts=(), kind=jnp.bfloat16):
    result = jax.random.normal(rng, extent, jnp.float32) * deviation
    if len(cuts) > 0:
        result = level_of(rng, extent, cuts, -0.22, 0.18) * result
    return jnp.clip(result, min=-reach, max=reach).astype(kind)


def setup_inputs(seed: int = 0) -> dict:
    key_list = jax.random.split(jax.random.key(seed), 13)
    vectors = centred(key_list[0], (COLS, ROWS), 1.0, 6.0, ((1, 64),))
    near_blocks = centred(key_list[1], (LEAVES, NEAR, LEAF, LEAF), (LEAF * NEAR) ** -0.5, 0.0625, ((0, 64), (1, 4)))
    near_cols = draw_near_cols(jax.random.fold_in(key_list[12], 71), 0)
    near_count = draw_near_count(jax.random.fold_in(key_list[12], 71), 0)
    col_basis = centred(key_list[4], (RANK, ROWS), LEAF ** -0.5, 0.375, ((1, 64),))
    row_basis = centred(key_list[5], (RANK, ROWS), (RANK * 16) ** -0.5, 0.1875, ((1, 64),))
    local_transfer = centred(key_list[6], (LOCAL_PARENTS, RANK, 2 * RANK), (2 * RANK) ** -0.5, 0.5, ((0, 64),))
    local_coupling = centred(key_list[7], (LOCAL_NODES, RANK, FAR * RANK), (FAR * RANK) ** -0.5, 0.25, ((0, 64), (2, 4)))
    local_partners = draw_local_partners(jax.random.fold_in(key_list[12], 71), 0)
    upper_transfer = centred(key_list[9], (UPPER, RANK, 2 * RANK), (2 * RANK) ** -0.5, 0.5)
    upper_coupling = centred(key_list[10], (UPPER, RANK, FAR * RANK), (FAR * RANK) ** -0.5, 0.25, ((2, 4),))
    upper_partners = draw_upper_partners(jax.random.fold_in(key_list[12], 71), 0)
    return {"vectors": vectors, "near_blocks": near_blocks, "near_cols": near_cols, "near_count": near_count, "col_basis": col_basis, "row_basis": row_basis, "local_transfer": local_transfer, "local_coupling": local_coupling, "local_partners": local_partners, "upper_transfer": upper_transfer, "upper_coupling": upper_coupling, "upper_partners": upper_partners}


def couple(matrices, coefs, partners):
    nodes = partners.shape[0]
    stacked = jnp.take(coefs, partners.reshape(-1), axis=0)
    stacked = stacked.reshape(nodes, -1, coefs.shape[2])
    return jnp.einsum('nab,nbc->nac', matrices.astype(jnp.float32), stacked.astype(jnp.float32))


def reference(vectors, near_blocks, near_cols, near_count, col_basis, row_basis, local_transfer, local_coupling, local_partners, upper_transfer, upper_coupling, upper_partners):
    highest = lax.Precision.HIGHEST
    leaves = LEAF_DEV * N_LEAF
    cols = vectors.shape[0]
    leaf_vectors = vectors.reshape(cols, leaves, LEAF)
    slot_ids = jnp.arange(NEAR, dtype=jnp.int32)

    def near_row(items):
        blocks, picks, count = items
        taken = jnp.take(leaf_vectors, picks, axis=1)
        taken = jnp.where((slot_ids < count)[None, :, None], taken, jnp.zeros_like(taken))
        return jnp.einsum('csa,sab->cb', taken.astype(jnp.float32), blocks.astype(jnp.float32))

    near_part = lax.map(near_row, (near_blocks, near_cols, near_count))

    basis = col_basis.reshape(RANK, leaves, LEAF).astype(jnp.float32)
    coef = jnp.einsum('ail,cil->iac', basis, leaf_vectors.astype(jnp.float32)).astype(jnp.bfloat16)
    levels_local = LEAF_DEV.bit_length() - 1
    couplings = local_coupling.reshape(N_LEAF, 2 * LEAF_DEV - 1, RANK, FAR * RANK)
    partners = local_partners.reshape(N_LEAF, 2 * LEAF_DEV - 1, FAR)
    transfers = local_transfer.reshape(N_LEAF, LEAF_DEV - 1, RANK, 2 * RANK)
    coefs = [coef]
    ups = []
    fields = []
    count = LEAF_DEV
    for level in range(levels_local + 1):
        start = 2 * LEAF_DEV - 2 * count
        mats = couplings[:, start:start + count].reshape(N_LEAF * count, RANK, FAR * RANK)
        picks = partners[:, start:start + count].reshape(N_LEAF * count, FAR)
        fields.append(couple(mats, coefs[-1], picks))
        if level < levels_local:
            half = count // 2
            pstart = LEAF_DEV - 2 * half
            emats = transfers[:, pstart:pstart + half].reshape(N_LEAF * half, RANK, 2 * RANK)
            ups.append(emats)
            pairs = coefs[-1].reshape(N_LEAF * half, 2 * RANK, cols)
            coefs.append(jnp.einsum('pab,pbc->pac', emats.astype(jnp.float32), pairs.astype(jnp.float32)).astype(jnp.bfloat16))
            count = half
    levels_upper = N_LEAF.bit_length() - 1
    count = N_LEAF
    start = 0
    for level in range(levels_upper):
        half = count // 2
        emats = upper_transfer[start:start + half]
        ups.append(emats)
        pairs = coefs[-1].reshape(half, 2 * RANK, cols)
        coefs.append(jnp.einsum('pab,pbc->pac', emats.astype(jnp.float32), pairs.astype(jnp.float32)).astype(jnp.bfloat16))
        fields.append(couple(upper_coupling[start:start + half], coefs[-1], upper_partners[start:start + half]))
        start = start + half
        count = half
    field = fields[-1]
    for level in range(len(ups) - 1, -1, -1):
        down = jnp.einsum('pba,pbc->pac', ups[level].astype(jnp.float32), field, precision=highest)
        field = fields[level] + down.reshape(-1, RANK, cols)
    rbasis = row_basis.reshape(RANK, leaves, LEAF).astype(jnp.float32)
    far = jnp.einsum('iac,ail->cil', field, rbasis, precision=highest)
    total = jnp.transpose(near_part, (1, 0, 2)) + far
    return total.astype(jnp.bfloat16).reshape(cols, leaves * LEAF)
```

```python
import functools

import jax
import jax.numpy as jnp
from jax import lax
from jax.experimental import pallas as pl
from jax.experimental.pallas import tpu as pltpu
from jax.sharding import PartitionSpec as P

F32, BF16 = jnp.float32, jnp.bfloat16
MESH = pl.DeviceIdType.MESH
ORDER = (2, 1, 3, 0)
START = (0, 8, 12, 14)
OFF = (None, 0, 32, 48, 56, 60, 62)


def nt(a, b):
    return lax.dot_general(a, b, (((1,), (1,)), ((), ())), preferred_element_type=F32)


def nn(a, b):
    return lax.dot_general(a, b, (((1,), (0,)), ((), ())), preferred_element_type=F32)


def row_of(level):
    return 3 * START[level] + (8 >> level)


def within(index, size):
    return jnp.minimum(jnp.maximum(index, 0), size - 1)


def low_half(shape):
    return lax.broadcasted_iota(jnp.int32, shape, 1) < 64


def paired(t):
    t = t.astype(F32)
    r = pltpu.roll(t, 64, 1)
    m = low_half(t.shape)
    z = jnp.zeros_like(t)
    top = jnp.concatenate([jnp.where(m, t, z), jnp.where(m, r, z)], axis=1)
    low = jnp.concatenate([jnp.where(m, z, r), jnp.where(m, z, t)], axis=1)
    return jnp.concatenate([top, low], axis=0).astype(BF16)


def split(f):
    hi = f.astype(BF16)
    lo = (f - hi.astype(F32)).astype(BF16)
    return hi, lo


def lowered(f, bd):
    hi, lo = split(f)
    return nn(jnp.concatenate([hi, lo], axis=1), jnp.concatenate([bd, bd], axis=0))


def kernel(
    vectors,
    near_blocks,
    near_cols,
    near_count,
    col_basis,
    row_basis,
    local_transfer,
    local_coupling,
    local_partners,
    upper_transfer,
    upper_coupling,
    upper_partners,
    out,
    wide0,
    wide1,
    wide2,
    wide3,
    nb,
    cb,
    rb,
    lt,
    lc,
    ut,
    ut1,
    ucp,
    ints,
    win,
    field,
    bdt,
    bdu,
    dnh,
    dnl,
    rootpair,
    gbuf,
    ups,
    send_buf,
    recv_buf,
    acc,
    loc_sem,
    own_sem,
    nb_sem,
    anc_sem,
    halo_send,
    halo_recv,
    coef_send,
    coef_recv,
    y_send,
    y_recv,
    i_send,
    i_recv,
    mate_sem,
    x_send,
    x_recv,
    z_send,
    z_recv,
    s_send,
    s_recv,
):
    l = lax.axis_index("leaf")
    y = lax.axis_index("near")
    left = lax.rem(l + 63, 64)
    right = lax.rem(l + 1, 64)
    core = lax.rem(l, 2)
    chip = l // 2
    x = lax.rem(chip, 4)
    z = chip // 4
    mate = l + 1 - 2 * core
    wides = (wide0, wide1, wide2, wide3)
    xs = [(z * 4 + lax.rem(x + d, 4)) * 2 + core for d in range(1, 4)]
    zs = [(lax.rem(z + d, 8) * 4 + x) * 2 + core for d in range(1, 8)]
    ys = [lax.rem(y + d, 4) for d in range(1, 4)]
    rows = [pl.multiple_of(lax.rem(y + d, 4) * 64, 64) for d in ORDER]
    ancestors = [None] + [OFF[m] + l // (1 << m) for m in range(1, 7)]

    def here(src, dst, sem):
        c = pltpu.make_async_copy(src, dst, sem)
        c.start()
        return c

    own = [
        [
            here(
                vectors.at[pl.ds(rows[p], 64), pl.ds(256 * i, 256)],
                wides[p].at[8 + i],
                own_sem.at[p, i],
            )
            for i in range(8)
        ]
        for p in range(4)
    ]
    get_cb = here(col_basis, cb, loc_sem.at[4])
    get_lt = here(local_transfer, lt, loc_sem.at[5])
    get_anc = [
        here(upper_coupling.at[ancestors[m]], ucp.at[0, m - 1], anc_sem.at[m - 1])
        for m in range(1, 7)
    ]
    get_ints = here(upper_partners, ints.at[0], loc_sem.at[6])
    get_ut1 = here(upper_transfer.at[chip], ut1, loc_sem.at[7])
    get_lc = here(local_coupling, lc, loc_sem.at[8])
    get_ut = here(upper_transfer.at[pl.ds(32, 31)], ut, loc_sem.at[9])
    get_rb = here(row_basis, rb, loc_sem.at[10])
    get_nb = [here(near_blocks.at[i], nb.at[i], nb_sem.at[i]) for i in range(8)]

    barrier = pltpu.get_barrier_semaphore()
    for t in [left, right] + xs + zs:
        pl.semaphore_signal(barrier, inc=1, device_id={"leaf": t}, device_id_type=MESH)
    for t in ys:
        pl.semaphore_signal(barrier, inc=1, device_id={"near": t}, device_id_type=MESH)

    get_lt.wait()
    for p in range(7):
        bdt[p] = paired(lt[p])
    for c in get_anc:
        c.wait()
    get_ints.wait()
    pl.semaphore_wait(barrier, 2 + 3 + 7 + 3)

    sends = []

    def remote(src, dst, s, r, target):
        c = pltpu.make_async_remote_copy(
            src_ref=src, dst_ref=dst, send_sem=s, recv_sem=r, device_id=target, device_id_type=MESH
        )
        c.start()
        sends.append(c)
        return c

    def halo(p):
        src = wides[p].at[pl.ds(8, 8)]
        return [
            remote(src, wides[p].at[pl.ds(0, 8)], halo_send.at[p, 0], halo_recv.at[p, 0], {"leaf": right}),
            remote(src, wides[p].at[pl.ds(16, 8)], halo_send.at[p, 1], halo_recv.at[p, 1], {"leaf": left}),
        ]

    for c in own[0]:
        c.wait()
    halos = [halo(0)]
    y_copies = []
    for d in range(1, 4):
        to = {"near": ys[d - 1]}
        y_copies.append(remote(ucp.at[0], ucp.at[d], y_send.at[d - 1], y_recv.at[d - 1], to))
        y_copies.append(remote(upper_partners, ints.at[d], i_send.at[d - 1], i_recv.at[d - 1], to))

    for p in range(1, 4):
        for c in own[p]:
            c.wait()
    get_cb.wait()
    for i in range(8):
        w = cb[:, 256 * i : 256 * (i + 1)]
        none = jnp.zeros_like(w)
        first = jnp.concatenate([wides[p][8 + i, 0:32, :] for p in range(4)], axis=0)
        second = jnp.concatenate([wides[p][8 + i, 32:64, :] for p in range(4)], axis=0)
        f = nt(first, jnp.concatenate([w, none], axis=0)) + nt(second, jnp.concatenate([none, w], axis=0))
        win[row_of(0) + i] = f.astype(BF16)
    for level in range(3):
        for g in range(4 >> level):
            c0 = row_of(level) + 2 * g
            pair = jnp.concatenate([win[c0], win[c0 + 1]], axis=1)
            win[row_of(level + 1) + g] = nt(pair, bdt[START[level + 1] - 8 + g]).astype(BF16)
    rootpair[core] = win[row_of(3), 96:128, :]
    mate_copy = remote(
        rootpair.at[core], rootpair.at[core], mate_sem.at[0], mate_sem.at[1], {"leaf": mate}
    )
    coef_copies = []
    for level in range(4):
        count = 8 >> level
        src = win.at[pl.ds(row_of(level), count)]
        for side, to in ((0, right), (1, left)):
            at = 3 * START[level] + 2 * side * count
            coef_copies.append(
                remote(src, win.at[pl.ds(at, count)], coef_send.at[level, side], coef_recv.at[level, side], {"leaf": to})
            )
    for p in range(1, 4):
        halos.append(halo(p))

    get_ut1.wait()
    bd1 = paired(ut1[...])
    mate_copy.wait_recv()
    gbuf[chip] = nt(jnp.concatenate([rootpair[0], rootpair[1]], axis=1), bd1).astype(BF16)
    x_copies = [
        remote(gbuf.at[chip], gbuf.at[chip], x_send.at[d], x_recv.at[d], {"leaf": xs[d]}) for d in range(3)
    ]

    get_ut.wait()
    for p in range(31):
        bdu[p] = paired(ut[p])

    def near_rows(p, i):
        total = jnp.zeros((64, 256), F32)
        for s in range(8):
            taken = wides[p][within(near_cols[i, s] - (l - 1) * 8, 24)]
            live = jnp.full((64, 256), near_count[i], jnp.int32) > y * 8 + s
            taken = jnp.where(live, taken, jnp.zeros_like(taken))
            total = total + nn(taken, nb[i, s])
        return total

    def far_rows(p, i):
        hi = dnh[i, 32 * p : 32 * p + 32, :].astype(F32)
        lo = dnl[i, 32 * p : 32 * p + 32, :].astype(F32)
        m = low_half((32, 128))
        none = jnp.zeros((32, 128), F32)
        top = jnp.concatenate([jnp.where(m, hi, none), jnp.where(m, lo, none)], axis=1)
        low = jnp.concatenate([jnp.where(m, none, hi), jnp.where(m, none, lo)], axis=1)
        f = jnp.concatenate([top, low], axis=0).astype(BF16)
        w = rb[:, pl.ds(pl.multiple_of(i * 256, 256), 256)]
        return nn(f, jnp.concatenate([w, w, w, w], axis=0))

    def lanes(i):
        return pl.ds(pl.multiple_of(i * 256, 256), 256)

    def local_fields():
        for level in range(4):
            count = 8 >> level
            for g in range(count):
                q = START[level] + g
                got = []
                for t in range(2):
                    w = within(local_partners[t, q] - (l - 1) * count, 3 * count)
                    got.append(win[3 * START[level] + w])
                field[q] = nt(jnp.concatenate(got, axis=1), paired(lc[q]))

    def descend(begin, end, extra):
        top = field[14, begin:end, :]
        downs = [top if extra is None else top + extra]
        for level in (2, 1, 0):
            lower = []
            for g, f in enumerate(downs):
                both = lowered(f, bdt[START[level + 1] - 8 + g])
                q = START[level] + 2 * g
                lower.append(both[:, 0:128] + field[q, begin:end, :])
                lower.append(both[:, 128:256] + field[q + 1, begin:end, :])
            downs = lower
        for i, f in enumerate(downs):
            hi, lo = split(f)
            dnh[i, begin:end, :] = hi
            dnl[i, begin:end, :] = lo

    def chunk(p):
        for c in halos[p]:
            c.wait_recv()
        if p == 0:
            for c in get_nb:
                c.wait()

        def step(i, carry):
            total = near_rows(p, i) + far_rows(p, i)
            if p < 3:
                send_buf[p, :, lanes(i)] = total.astype(BF16)
            else:
                acc[:, lanes(i)] = total
            return carry

        lax.fori_loop(0, 8, step, 0)
        if p < 3:
            d = ORDER[p]
            return remote(
                send_buf.at[p], recv_buf.at[p], s_send.at[p], s_recv.at[p], {"near": ys[d - 1]}
            )

    for c in x_copies:
        c.wait_recv()
    plane = pl.ds(z * 4, 4)
    z_copies = [
        remote(gbuf.at[plane], gbuf.at[plane], z_send.at[d], z_recv.at[d], {"leaf": zs[d]}) for d in range(7)
    ]

    for c in coef_copies:
        c.wait_recv()
    get_lc.wait()
    local_fields()
    descend(0, 96, None)
    get_rb.wait()
    sums = [chunk(0), chunk(1)]

    for c in z_copies:
        c.wait_recv()
    for m in range(2, 7):
        for p in range(64 >> m):
            if m == 2:
                pair = [gbuf[2 * p], gbuf[2 * p + 1]]
            else:
                c0 = OFF[m - 1] - 32 + 2 * p
                pair = [ups[c0], ups[c0 + 1]]
            row = OFF[m] - 32 + p
            ups[row] = nt(jnp.concatenate(pair, axis=1), bdu[row]).astype(BF16)
    for c in y_copies:
        c.wait_recv()
    down = None
    for m in range(6, 0, -1):
        f = None
        for d in range(4):
            got = []
            for t in range(2):
                q = within(ints[d, t, ancestors[m]], 64 >> m)
                got.append(gbuf[q] if m == 1 else ups[OFF[m] - 32 + q])
            part = nt(jnp.concatenate(got, axis=1), paired(ucp[d, m - 1]))
            f = part if f is None else f + part
        if down is not None:
            f = f + down
        both = lowered(f, bd1 if m == 1 else bdu[ancestors[m] - 32])
        even = lax.rem(l // (1 << (m - 1)), 2) == 0
        down = jnp.where(even, both[:, 0:128], both[:, 128:256])
    descend(96, 128, down)

    sums.append(chunk(2))
    chunk(3)
    for c in sums:
        c.wait_recv()
    out[...] = (
        acc[...] + recv_buf[0].astype(F32) + recv_buf[1].astype(F32) + recv_buf[2].astype(F32)
    ).astype(BF16)
    for c in sends:
        c.wait_send()


def local(
    vectors,
    near_blocks,
    near_cols,
    near_count,
    col_basis,
    row_basis,
    local_transfer,
    local_coupling,
    local_partners,
    upper_transfer,
    upper_coupling,
    upper_partners,
):
    anywhere = pl.BlockSpec(memory_space=pl.ANY)
    scalars = pl.BlockSpec(memory_space=pltpu.SMEM)
    dma = pltpu.SemaphoreType.DMA
    vm = pltpu.VMEM
    return pl.pallas_call(
        kernel,
        out_shape=jax.ShapeDtypeStruct((64, 2048), BF16),
        in_specs=[
            anywhere,
            anywhere,
            scalars,
            scalars,
            anywhere,
            anywhere,
            anywhere,
            anywhere,
            scalars,
            anywhere,
            anywhere,
            anywhere,
        ],
        out_specs=pl.BlockSpec(memory_space=pltpu.VMEM),
        scratch_shapes=[vm((24, 64, 256), BF16) for _ in range(4)]
        + [
            vm((8, 8, 256, 256), BF16),
            vm((64, 2048), BF16),
            vm((64, 2048), BF16),
            vm((7, 64, 128), BF16),
            vm((15, 64, 128), BF16),
            vm((31, 64, 128), BF16),
            vm((64, 128), BF16),
            vm((4, 6, 64, 128), BF16),
            pltpu.SMEM((4, 2, 63), jnp.int32),
            vm((45, 128, 128), BF16),
            vm((15, 128, 128), F32),
            vm((7, 128, 256), BF16),
            vm((31, 128, 256), BF16),
            vm((8, 128, 128), BF16),
            vm((8, 128, 128), BF16),
            vm((2, 32, 128), BF16),
            vm((32, 32, 128), BF16),
            vm((31, 32, 128), BF16),
            vm((3, 64, 2048), BF16),
            vm((3, 64, 2048), BF16),
            vm((64, 2048), F32),
            dma((11,)),
            dma((4, 8)),
            dma((8,)),
            dma((6,)),
            dma((4, 2)),
            dma((4, 2)),
            dma((4, 2)),
            dma((4, 2)),
            dma((3,)),
            dma((3,)),
            dma((3,)),
            dma((3,)),
            dma((2,)),
            dma((3,)),
            dma((3,)),
            dma((7,)),
            dma((7,)),
            dma((3,)),
            dma((3,)),
        ],
        compiler_params=pltpu.CompilerParams(
            collective_id=0, has_side_effects=True, vmem_limit_bytes=63 * 1024 * 1024
        ),
        name="h2",
    )(
        vectors,
        near_blocks,
        near_cols,
        near_count,
        col_basis,
        row_basis,
        local_transfer,
        local_coupling,
        local_partners.T,
        upper_transfer,
        upper_coupling,
        upper_partners.T,
    )


def solution(mesh):
    return jax.shard_map(
        local,
        mesh=mesh,
        in_specs=(
            P(None, "leaf"),
            P("leaf", "near", None, None),
            P("leaf", "near"),
            P("leaf"),
            P(None, "leaf"),
            P(None, "leaf"),
            P("leaf", None, None),
            P("leaf", None, "near"),
            P("leaf", "near"),
            P(),
            P(None, None, "near"),
            P(None, "near"),
        ),
        out_specs=P("near", "leaf"),
        check_vma=False,
    )
```

```python
import functools

import jax
import jax.numpy as jnp
from jax import lax
from jax.experimental import pallas as pl
from jax.experimental.pallas import tpu as pltpu
from jax.sharding import PartitionSpec as P

F32, BF16 = jnp.float32, jnp.bfloat16
MESH = pl.DeviceIdType.MESH
ORDER = (1, 3, 2, 0)
START = (0, 8, 12, 14)
OFF = (None, 0, 32, 48, 56, 60, 62)


def nt(a, b):
    return lax.dot_general(a, b, (((1,), (1,)), ((), ())), preferred_element_type=F32)


def nn(a, b):
    return lax.dot_general(a, b, (((1,), (0,)), ((), ())), preferred_element_type=F32)


def within(index, size):
    return jnp.minimum(jnp.maximum(index, 0), size - 1)


def low_half(shape):
    return lax.broadcasted_iota(jnp.int32, shape, 1) < 64


def paired(t):
    t = t.astype(F32)
    r = pltpu.roll(t, 64, 1)
    m = low_half(t.shape)
    z = jnp.zeros_like(t)
    top = jnp.concatenate([jnp.where(m, t, z), jnp.where(m, r, z)], axis=1)
    low = jnp.concatenate([jnp.where(m, z, r), jnp.where(m, z, t)], axis=1)
    return jnp.concatenate([top, low], axis=0).astype(BF16)


def split(f):
    hi = f.astype(BF16)
    lo = (f - hi.astype(F32)).astype(BF16)
    return hi, lo


def lowered(f, bd):
    hi, lo = split(f)
    return nn(jnp.concatenate([hi, lo], axis=1), jnp.concatenate([bd, bd], axis=0))


def kernel(
    vectors,
    near_blocks,
    near_cols,
    near_count,
    col_basis,
    row_basis,
    local_transfer,
    local_coupling,
    local_partners,
    upper_transfer,
    upper_coupling,
    upper_partners,
    out,
    wide0,
    wide1,
    wide2,
    wide3,
    nb,
    cb,
    rb,
    rb4,
    lt,
    lc,
    ut,
    ut1,
    ucp,
    ints,
    win,
    field,
    bdt,
    bdu,
    unfolded,
    rootpair,
    gbuf,
    ups,
    down_send,
    downs,
    hop_send,
    hop_recv,
    send_buf,
    recv_buf,
    acc,
    loc_sem,
    own_sem,
    nb_sem,
    anc_sem,
    halo_send,
    halo_recv,
    coef_send,
    coef_recv,
    y_send,
    y_recv,
    i_send,
    i_recv,
    share_send,
    share_recv,
    mate_sem,
    down_sem,
    ucp_sem,
    x_send,
    x_recv,
    z_send,
    z_recv,
    s_send,
    s_recv,
):
    l = lax.axis_index("leaf")
    y = lax.axis_index("near")
    core = lax.rem(l, 2)
    outer = lax.rem(l + 63 + 2 * core, 64)
    outer_side = 2 - 2 * core
    mate_side = 2 * core
    chip = l // 2
    x = lax.rem(chip, 4)
    z = chip // 4
    mate = l + 1 - 2 * core
    wides = (wide0, wide1, wide2, wide3)
    xs = [(z * 4 + lax.rem(x + d, 4)) * 2 + core for d in range(1, 4)]
    zs = [(lax.rem(z + d, 8) * 4 + x) * 2 + core for d in range(1, 8)]
    ys = [lax.rem(y + d, 4) for d in range(1, 4)]
    rows = [pl.multiple_of(lax.rem(y + d, 4) * 64, 64) for d in ORDER]
    ancestors = [None] + [OFF[m] + l // (1 << m) for m in range(1, 7)]

    barrier = pltpu.get_barrier_semaphore()
    for t in [outer, mate] + xs + zs:
        pl.semaphore_signal(barrier, inc=1, device_id={"leaf": t}, device_id_type=MESH)
    for t in ys:
        pl.semaphore_signal(barrier, inc=1, device_id={"near": t}, device_id_type=MESH)

    def here(src, dst, sem):
        c = pltpu.make_async_copy(src, dst, sem)
        c.start()
        return c

    own = [
        [
            here(
                vectors.at[pl.ds(rows[p], 64), pl.ds(256 * i, 256)],
                wides[p].at[8 + i],
                own_sem.at[p, i],
            )
            for i in range(8)
        ]
        for p in range(4)
    ]
    get_cb = here(col_basis, cb, loc_sem.at[4])
    get_lt = here(local_transfer, lt, loc_sem.at[5])
    get_anc = [
        here(upper_coupling.at[ancestors[m]], ucp.at[0, m - 1], anc_sem.at[m - 1])
        for m in range(1, 7)
    ]
    get_ints = here(upper_partners, ints.at[0], loc_sem.at[6])
    get_ut1 = here(upper_transfer.at[chip], ut1, loc_sem.at[7])
    get_lc = here(local_coupling, lc, loc_sem.at[8])
    get_ut = here(upper_transfer.at[pl.ds(32, 31)], ut, loc_sem.at[9])
    get_rb = here(row_basis, rb, loc_sem.at[10])
    get_nb = [here(near_blocks.at[i], nb.at[i], nb_sem.at[i]) for i in range(8)]

    sends = []

    def remote(src, dst, s, r, target):
        c = pltpu.make_async_remote_copy(
            src_ref=src, dst_ref=dst, send_sem=s, recv_sem=r, device_id=target, device_id_type=MESH
        )
        c.start()
        sends.append(c)
        return c

    def halo(p, to, side, k):
        return remote(
            wides[p].at[pl.ds(8, 8)], wides[p].at[pl.ds(8 * side, 8)], halo_send.at[p, k], halo_recv.at[p, k], {"leaf": to}
        )

    get_lt.wait()
    for p in range(7):
        bdt[p] = paired(lt[p])
    for p in range(4):
        for c in own[p]:
            c.wait()
    get_cb.wait()
    for i in range(8):
        w = cb[:, 256 * i : 256 * (i + 1)]
        none = jnp.zeros_like(w)
        first = jnp.concatenate([wides[p][8 + i, 0:32, :] for p in range(4)], axis=0)
        second = jnp.concatenate([wides[p][8 + i, 32:64, :] for p in range(4)], axis=0)
        f = nt(first, jnp.concatenate([w, none], axis=0)) + nt(second, jnp.concatenate([none, w], axis=0))
        win[1, i] = f.astype(BF16)
    for level in range(3):
        for g in range(4 >> level):
            c0 = START[level] + 2 * g
            pair = jnp.concatenate([win[1, c0], win[1, c0 + 1]], axis=1)
            win[1, START[level + 1] + g] = nt(pair, bdt[START[level + 1] - 8 + g]).astype(BF16)
    mine = pl.ds(pl.multiple_of(96 + 16 * core, 16), 16)
    other = pl.ds(pl.multiple_of(112 - 16 * core, 16), 16)
    rootpair[core] = win[1, 14, mine, :]
    get_rb.wait()
    for c in get_anc:
        c.wait()
    get_ints.wait()

    pl.semaphore_wait(barrier, 2 + 3 + 7 + 3)
    mate_copy = remote(
        win.at[1, 14, other], rootpair.at[core], mate_sem.at[0], mate_sem.at[1], {"leaf": mate}
    )
    y_copies, i_copies = [], []
    some = pl.ds(3 * core, 3)
    for d in range(1, 4):
        to = {"near": ys[d - 1]}
        y_copies.append(remote(ucp.at[0, some], ucp.at[d, some], y_send.at[d - 1], y_recv.at[d - 1], to))
        i_copies.append(remote(upper_partners, ints.at[d], i_send.at[d - 1], i_recv.at[d - 1], to))
    outer_coefs = remote(
        win.at[1, :, pl.ds(64, 64)],
        win.at[outer_side, :, pl.ds(64, 64)],
        coef_send.at[0],
        coef_recv.at[0],
        {"leaf": outer},
    )
    outer_halos = {2: halo(2, outer, outer_side, 0)}
    mate_coefs = remote(win.at[1], win.at[mate_side], coef_send.at[1], coef_recv.at[1], {"leaf": mate})
    mate_halos = [halo(p, mate, mate_side, 1) for p in range(4)]

    get_ut1.wait()
    bd1 = paired(ut1[...])
    mate_copy.wait_recv()
    gbuf[chip] = nt(jnp.concatenate([rootpair[0], rootpair[1]], axis=1), bd1).astype(BF16)
    x_copies = [
        remote(gbuf.at[chip], gbuf.at[chip], x_send.at[d], x_recv.at[d], {"leaf": xs[d]}) for d in range(3)
    ]
    outer_coefs.wait_recv()
    got = 2 * core
    shares = [
        remote(
            win.at[got, :, pl.ds(96, 32)],
            win.at[got, :, pl.ds(32 * p, 32)],
            share_send.at[p],
            share_recv.at[p],
            {"near": ys[3 - ORDER[p]]},
        )
        for p in range(2)
    ]
    outer_halos[0] = halo(0, outer, outer_side, 0)

    for i in range(8):
        w = rb[:, 256 * i : 256 * (i + 1)]
        rb4[i] = jnp.concatenate([w, w, w, w], axis=0)
    get_ut.wait()
    for p in range(31):
        bdu[p] = paired(ut[p])

    def near_rows(p, i):
        total = jnp.zeros((64, 256), F32)
        for s in range(8):
            taken = wides[p][within(near_cols[i, s] - (l - 1) * 8, 24)]
            live = jnp.full((64, 256), near_count[i], jnp.int32) > y * 8 + s
            taken = jnp.where(live, taken, jnp.zeros_like(taken))
            total = total + nn(taken, nb[i, s])
        return total

    def far_rows(p, i):
        return nn(unfolded[p, i], rb4[i])

    def lanes(i):
        return pl.ds(pl.multiple_of(i * 256, 256), 256)

    def local_fields():
        for level in range(4):
            count = 8 >> level
            for g in range(count):
                q = START[level] + g
                got = []
                for t in range(2):
                    w = within(local_partners[t, q] - (l - 1) * count, 3 * count)
                    side = lax.shift_right_logical(w, 3 - level)
                    got.append(win[side, START[level] + w - side * count])
                field[q] = nt(jnp.concatenate(got, axis=1), paired(lc[q]))

    def descend(begin, end, extra):
        top = field[14, begin:end, :]
        downs = [top if extra is None else top + extra]
        for level in (2, 1, 0):
            lower = []
            for g, f in enumerate(downs):
                both = lowered(f, bdt[START[level + 1] - 8 + g])
                q = START[level] + 2 * g
                lower.append(both[:, 0:128] + field[q, begin:end, :])
                lower.append(both[:, 128:256] + field[q + 1, begin:end, :])
            downs = lower
        for i, f in enumerate(downs):
            for p in range(begin // 32, end // 32):
                rows32 = f[32 * p - begin : 32 * p - begin + 32, :]
                none = jnp.zeros_like(rows32)
                m = low_half((32, 128))
                both = jnp.concatenate([jnp.where(m, rows32, none), jnp.where(m, none, rows32)], axis=0)
                hi, lo = split(both)
                unfolded[p, i] = jnp.concatenate([hi, lo], axis=1)

    def half(p, h):
        def step(k, carry):
            i = 4 * h + k
            near = acc[:, lanes(i)] if p == 2 else near_rows(p, i)
            total = near + far_rows(p, i)
            if (p, h) == (0, 0):
                total = total + hop_recv[0, :, lanes(k)].astype(F32)
            if (p, h) == (1, 1):
                total = total + hop_recv[1, :, lanes(k)].astype(F32)
            if p == 2:
                hop_send[h, :, lanes(k)] = total.astype(BF16)
            elif p < 2:
                send_buf[p, h, :, lanes(k)] = total.astype(BF16)
            else:
                acc[:, lanes(i)] = total
            return carry

        lax.fori_loop(0, 4, step, 0, unroll=2)
        if p == 2:
            to = ys[0] if h == 0 else ys[2]
            return remote(hop_send.at[h], hop_recv.at[h], s_send.at[2, h], s_recv.at[2, h], {"near": to})
        if p < 2:
            to = ys[0] if p == 0 else ys[2]
            return remote(
                send_buf.at[p, h], recv_buf.at[p, h], s_send.at[p, h], s_recv.at[p, h], {"near": to}
            )

    for c in x_copies:
        c.wait_recv()
    plane = pl.ds(z * 4, 4)
    z_copies = [
        remote(gbuf.at[plane], gbuf.at[plane], z_send.at[d], z_recv.at[d], {"leaf": zs[d]}) for d in range(7)
    ]

    for c in y_copies:
        c.wait_recv()
    ucp_copy = remote(
        ucp.at[pl.ds(1, 3), some], ucp.at[pl.ds(1, 3), some], ucp_sem.at[0], ucp_sem.at[1], {"leaf": mate}
    )

    def arrive(p):
        outer_halos[p].wait_recv()
        mate_halos[p].wait_recv()

    arrive(2)
    outer_halos[1] = halo(1, outer, outer_side, 0)
    for c in get_nb:
        c.wait()

    def near_step(i, carry):
        acc[:, lanes(i)] = near_rows(2, i)
        return carry

    lax.fori_loop(0, 8, near_step, 0, unroll=2)
    mate_coefs.wait_recv()
    for c in shares:
        c.wait_recv()
    get_lc.wait()
    local_fields()
    descend(0, 96, None)
    hops = [half(2, 0), half(2, 1)]

    arrive(0)
    outer_halos[3] = halo(3, outer, outer_side, 0)
    sums = [half(0, 1)]
    hops[0].wait_recv()
    sums.append(half(0, 0))

    arrive(1)
    sums.append(half(1, 0))
    hops[1].wait_recv()
    sums.append(half(1, 1))

    for c in z_copies:
        c.wait_recv()
    for m in range(2, 7):
        for p in range(64 >> m):
            if m == 2:
                pair = [gbuf[2 * p], gbuf[2 * p + 1]]
            else:
                c0 = OFF[m - 1] - 32 + 2 * p
                pair = [ups[c0], ups[c0 + 1]]
            row = OFF[m] - 32 + p
            ups[row] = nt(jnp.concatenate(pair, axis=1), bdu[row]).astype(BF16)
    ucp_copy.wait_recv()
    for c in i_copies:
        c.wait_recv()
    down = None
    for m in range(6, 0, -1):
        f = None
        for d in range(4):
            got = []
            for t in range(2):
                q = within(ints[d, t, ancestors[m]], 64 >> m)
                got.append(gbuf[q] if m == 1 else ups[OFF[m] - 32 + q])
            part = nt(jnp.concatenate(got, axis=1), paired(ucp[d, m - 1]))
            f = part if f is None else f + part
        if down is not None:
            f = f + down
        both = lowered(f, bd1 if m == 1 else bdu[ancestors[m] - 32])
        even = lax.rem(l // (1 << (m - 1)), 2) == 0
        down = jnp.where(even, both[:, 0:128], both[:, 128:256])
        if m == 1:
            down_send[...] = jnp.where(even, both[:, 128:256], both[:, 0:128])
            downs[core] = down
    down_copy = remote(down_send, downs.at[core], down_sem.at[0], down_sem.at[1], {"leaf": mate})
    down_copy.wait_recv()
    descend(96, 128, jnp.concatenate([downs[0], downs[1]], axis=0))

    arrive(3)
    half(3, 0)
    half(3, 1)
    for c in sums:
        c.wait_recv()
    for h in range(2):
        at = pl.ds(1024 * h, 1024)
        out[:, at] = (
            acc[:, at] + recv_buf[0, h].astype(F32) + recv_buf[1, h].astype(F32)
        ).astype(BF16)
    for c in sends:
        c.wait_send()


def local(
    vectors,
    near_blocks,
    near_cols,
    near_count,
    col_basis,
    row_basis,
    local_transfer,
    local_coupling,
    local_partners,
    upper_transfer,
    upper_coupling,
    upper_partners,
):
    anywhere = pl.BlockSpec(memory_space=pl.ANY)
    scalars = pl.BlockSpec(memory_space=pltpu.SMEM)
    dma = pltpu.SemaphoreType.DMA
    vm = pltpu.VMEM
    return pl.pallas_call(
        kernel,
        out_shape=jax.ShapeDtypeStruct((64, 2048), BF16),
        in_specs=[
            anywhere,
            anywhere,
            scalars,
            scalars,
            anywhere,
            anywhere,
            anywhere,
            anywhere,
            scalars,
            anywhere,
            anywhere,
            anywhere,
        ],
        out_specs=pl.BlockSpec(memory_space=pltpu.VMEM),
        scratch_shapes=[vm((24, 64, 256), BF16) for _ in range(4)]
        + [
            vm((8, 8, 256, 256), BF16),
            vm((64, 2048), BF16),
            vm((64, 2048), BF16),
            vm((8, 256, 256), BF16),
            vm((7, 64, 128), BF16),
            vm((15, 64, 128), BF16),
            vm((31, 64, 128), BF16),
            vm((64, 128), BF16),
            vm((4, 6, 64, 128), BF16),
            pltpu.SMEM((4, 2, 63), jnp.int32),
            vm((3, 15, 128, 128), BF16),
            vm((15, 128, 128), F32),
            vm((7, 128, 256), BF16),
            vm((31, 128, 256), BF16),
            vm((4, 8, 64, 256), BF16),
            vm((2, 16, 128), BF16),
            vm((32, 16, 128), BF16),
            vm((31, 16, 128), BF16),
            vm((16, 128), F32),
            vm((2, 16, 128), F32),
            vm((2, 64, 1024), BF16),
            vm((2, 64, 1024), BF16),
            vm((2, 2, 64, 1024), BF16),
            vm((2, 2, 64, 1024), BF16),
            vm((64, 2048), F32),
            dma((11,)),
            dma((4, 8)),
            dma((8,)),
            dma((6,)),
            dma((4, 2)),
            dma((4, 2)),
            dma((2,)),
            dma((2,)),
            dma((3,)),
            dma((3,)),
            dma((3,)),
            dma((3,)),
            dma((2,)),
            dma((2,)),
            dma((2,)),
            dma((2,)),
            dma((2,)),
            dma((3,)),
            dma((3,)),
            dma((7,)),
            dma((7,)),
            dma((3, 2)),
            dma((3, 2)),
        ],
        compiler_params=pltpu.CompilerParams(
            collective_id=0, has_side_effects=True, vmem_limit_bytes=63 * 1024 * 1024
        ),
        name="h2",
    )(
        vectors,
        near_blocks,
        near_cols,
        near_count,
        col_basis,
        row_basis,
        local_transfer,
        local_coupling,
        local_partners.T,
        upper_transfer,
        upper_coupling,
        upper_partners.T,
    )


def solution(mesh):
    return jax.shard_map(
        local,
        mesh=mesh,
        in_specs=(
            P(None, "leaf"),
            P("leaf", "near", None, None),
            P("leaf", "near"),
            P("leaf"),
            P(None, "leaf"),
            P(None, "leaf"),
            P("leaf", None, None),
            P("leaf", None, "near"),
            P("leaf", "near"),
            P(),
            P(None, None, "near"),
            P(None, "near"),
        ),
        out_specs=P("near", "leaf"),
        check_vma=False,
    )
```

```python
import functools

import jax
import jax.numpy as jnp
from jax import lax
from jax.experimental import pallas as pl
from jax.experimental.pallas import tpu as pltpu
from jax.sharding import PartitionSpec as P

F32, BF16 = jnp.float32, jnp.bfloat16
MESH = pl.DeviceIdType.MESH
ORDER = (1, 3, 2, 0)
START = (0, 8, 12, 14)
OFF = (None, 0, 32, 48, 56, 60, 62)


def nt(a, b):
    return lax.dot_general(a, b, (((1,), (1,)), ((), ())), preferred_element_type=F32)


def nn(a, b):
    return lax.dot_general(a, b, (((1,), (0,)), ((), ())), preferred_element_type=F32)


def within(index, size):
    return jnp.minimum(jnp.maximum(index, 0), size - 1)


def low_half(shape):
    return lax.broadcasted_iota(jnp.int32, shape, 1) < 64


def paired(t):
    t = t.astype(F32)
    r = pltpu.roll(t, 64, 1)
    m = low_half(t.shape)
    z = jnp.zeros_like(t)
    top = jnp.concatenate([jnp.where(m, t, z), jnp.where(m, r, z)], axis=1)
    low = jnp.concatenate([jnp.where(m, z, r), jnp.where(m, z, t)], axis=1)
    return jnp.concatenate([top, low], axis=0).astype(BF16)


def split(f):
    hi = f.astype(BF16)
    lo = (f - hi.astype(F32)).astype(BF16)
    return hi, lo


def lowered(f, bd):
    hi, lo = split(f)
    return nn(jnp.concatenate([hi, lo], axis=1), jnp.concatenate([bd, bd], axis=0))


def kernel(
    vectors,
    near_blocks,
    near_cols,
    near_count,
    col_basis,
    row_basis,
    local_transfer,
    local_coupling,
    local_partners,
    upper_transfer,
    upper_coupling,
    upper_partners,
    out,
    wide0,
    wide1,
    wide2,
    wide3,
    nb,
    cb,
    rb,
    rb4,
    lt,
    lc,
    ut,
    ut1,
    ucp,
    ints,
    win,
    field,
    bdt,
    bdu,
    unfolded,
    rootpair,
    gbuf,
    ups,
    down_send,
    downs,
    hop_send,
    hop_recv,
    send_buf,
    recv_buf,
    acc,
    loc_sem,
    own_sem,
    nb_sem,
    anc_sem,
    halo_send,
    halo_recv,
    coef_send,
    coef_recv,
    y_send,
    y_recv,
    i_send,
    i_recv,
    share_send,
    share_recv,
    mate_sem,
    down_sem,
    ucp_sem,
    x_send,
    x_recv,
    z_send,
    z_recv,
    s_send,
    s_recv,
):
    l = lax.axis_index("leaf")
    y = lax.axis_index("near")
    core = lax.rem(l, 2)
    outer = lax.rem(l + 63 + 2 * core, 64)
    outer_side = 2 - 2 * core
    mate_side = 2 * core
    chip = l // 2
    x = lax.rem(chip, 4)
    z = chip // 4
    mate = l + 1 - 2 * core
    wides = (wide0, wide1, wide2, wide3)
    xs = [(z * 4 + lax.rem(x + d, 4)) * 2 + core for d in range(1, 4)]
    zs = [(lax.rem(z + d, 8) * 4 + x) * 2 + core for d in range(1, 8)]
    ys = [lax.rem(y + d, 4) for d in range(1, 4)]
    rows = [pl.multiple_of(lax.rem(y + d, 4) * 64, 64) for d in ORDER]
    ancestors = [None] + [OFF[m] + l // (1 << m) for m in range(1, 7)]

    barrier = pltpu.get_barrier_semaphore()
    for t in [outer, mate] + xs + zs:
        pl.semaphore_signal(barrier, inc=1, device_id={"leaf": t}, device_id_type=MESH)
    for t in ys:
        pl.semaphore_signal(barrier, inc=1, device_id={"near": t}, device_id_type=MESH)

    def here(src, dst, sem):
        c = pltpu.make_async_copy(src, dst, sem)
        c.start()
        return c

    own = [
        [
            here(
                vectors.at[pl.ds(rows[p], 64), pl.ds(256 * i, 256)],
                wides[p].at[8 + i],
                own_sem.at[p, i],
            )
            for i in range(8)
        ]
        for p in range(4)
    ]
    get_cb = here(col_basis, cb, loc_sem.at[4])
    get_lt = here(local_transfer, lt, loc_sem.at[5])
    get_anc = [
        here(upper_coupling.at[ancestors[m]], ucp.at[0, m - 1], anc_sem.at[m - 1])
        for m in range(1, 7)
    ]
    get_ints = here(upper_partners, ints.at[0], loc_sem.at[6])
    get_ut1 = here(upper_transfer.at[chip], ut1, loc_sem.at[7])
    get_lc = here(local_coupling, lc, loc_sem.at[8])
    get_ut = here(upper_transfer.at[pl.ds(32, 31)], ut, loc_sem.at[9])
    get_rb = here(row_basis, rb, loc_sem.at[10])
    get_nb = [here(near_blocks.at[i], nb.at[i], nb_sem.at[i]) for i in range(8)]

    sends = []

    def remote(src, dst, s, r, target):
        c = pltpu.make_async_remote_copy(
            src_ref=src, dst_ref=dst, send_sem=s, recv_sem=r, device_id=target, device_id_type=MESH
        )
        c.start()
        sends.append(c)
        return c

    def halo(p, to, side, k):
        return remote(
            wides[p].at[pl.ds(8, 8)], wides[p].at[pl.ds(8 * side, 8)], halo_send.at[p, k], halo_recv.at[p, k], {"leaf": to}
        )

    get_lt.wait()
    for p in range(7):
        bdt[p] = paired(lt[p])
    for p in range(4):
        for c in own[p]:
            c.wait()
    get_cb.wait()
    for i in range(8):
        w = cb[:, 256 * i : 256 * (i + 1)]
        none = jnp.zeros_like(w)
        first = jnp.concatenate([wides[p][8 + i, 0:32, :] for p in range(4)], axis=0)
        second = jnp.concatenate([wides[p][8 + i, 32:64, :] for p in range(4)], axis=0)
        f = nt(first, jnp.concatenate([w, none], axis=0)) + nt(second, jnp.concatenate([none, w], axis=0))
        win[1, i] = f.astype(BF16)
    for level in range(3):
        for g in range(4 >> level):
            c0 = START[level] + 2 * g
            pair = jnp.concatenate([win[1, c0], win[1, c0 + 1]], axis=1)
            win[1, START[level + 1] + g] = nt(pair, bdt[START[level + 1] - 8 + g]).astype(BF16)
    mine = pl.ds(pl.multiple_of(96 + 16 * core, 16), 16)
    other = pl.ds(pl.multiple_of(112 - 16 * core, 16), 16)
    rootpair[core] = win[1, 14, mine, :]
    get_rb.wait()
    for c in get_anc:
        c.wait()
    get_ints.wait()

    pl.semaphore_wait(barrier, 2 + 3 + 7 + 3)
    mate_copy = remote(
        win.at[1, 14, other], rootpair.at[core], mate_sem.at[0], mate_sem.at[1], {"leaf": mate}
    )
    y_copies, i_copies = [], []
    some = pl.ds(3 * core, 3)
    for d in range(1, 4):
        to = {"near": ys[d - 1]}
        y_copies.append(remote(ucp.at[0, some], ucp.at[d, some], y_send.at[d - 1], y_recv.at[d - 1], to))
        i_copies.append(remote(upper_partners, ints.at[d], i_send.at[d - 1], i_recv.at[d - 1], to))
    outer_coefs = remote(
        win.at[1, :, pl.ds(64, 64)],
        win.at[outer_side, :, pl.ds(64, 64)],
        coef_send.at[0],
        coef_recv.at[0],
        {"leaf": outer},
    )
    outer_halos = {}
    mate_coefs = remote(win.at[1], win.at[mate_side], coef_send.at[1], coef_recv.at[1], {"leaf": mate})
    mate_halos = [halo(p, mate, mate_side, 1) for p in range(4)]

    get_ut1.wait()
    bd1 = paired(ut1[...])
    mate_copy.wait_recv()
    gbuf[chip] = nt(jnp.concatenate([rootpair[0], rootpair[1]], axis=1), bd1).astype(BF16)
    x_copies = [
        remote(gbuf.at[chip], gbuf.at[chip], x_send.at[d], x_recv.at[d], {"leaf": xs[d]}) for d in range(3)
    ]
    outer_halos[2] = halo(2, outer, outer_side, 0)
    outer_coefs.wait_recv()
    got = 2 * core
    shares = [
        remote(
            win.at[got, :, pl.ds(96, 32)],
            win.at[got, :, pl.ds(32 * p, 32)],
            share_send.at[p],
            share_recv.at[p],
            {"near": ys[3 - ORDER[p]]},
        )
        for p in range(2)
    ]

    for i in range(8):
        w = rb[:, 256 * i : 256 * (i + 1)]
        rb4[i] = jnp.concatenate([w, w, w, w], axis=0)
    get_ut.wait()
    for p in range(31):
        bdu[p] = paired(ut[p])

    def near_rows(chunks, i):
        total = jnp.zeros((64 * len(chunks), 256), F32)
        for t in range(8):
            j = within(near_cols[i, t] - (l - 1) * 8, 24)
            taken = jnp.concatenate([wides[p][j] for p in chunks], axis=0)
            live = jnp.full(taken.shape, near_count[i], jnp.int32) > y * 8 + t
            taken = jnp.where(live, taken, jnp.zeros_like(taken))
            total = total + nn(taken, nb[i, t])
        return total

    def far_rows(p, i):
        return nn(unfolded[p, i], rb4[i])

    def lanes(i):
        return pl.ds(pl.multiple_of(i * 256, 256), 256)

    def local_fields():
        for level in range(4):
            count = 8 >> level
            for g in range(count):
                q = START[level] + g
                got = []
                for t in range(2):
                    w = within(local_partners[t, q] - (l - 1) * count, 3 * count)
                    side = lax.shift_right_logical(w, 3 - level)
                    got.append(win[side, START[level] + w - side * count])
                field[q] = nt(jnp.concatenate(got, axis=1), paired(lc[q]))

    def descend(begin, end, extra):
        top = field[14, begin:end, :]
        downs = [top if extra is None else top + extra]
        for level in (2, 1, 0):
            lower = []
            for g, f in enumerate(downs):
                both = lowered(f, bdt[START[level + 1] - 8 + g])
                q = START[level] + 2 * g
                lower.append(both[:, 0:128] + field[q, begin:end, :])
                lower.append(both[:, 128:256] + field[q + 1, begin:end, :])
            downs = lower
        for i, f in enumerate(downs):
            for p in range(begin // 32, end // 32):
                rows32 = f[32 * p - begin : 32 * p - begin + 32, :]
                none = jnp.zeros_like(rows32)
                m = low_half((32, 128))
                both = jnp.concatenate([jnp.where(m, rows32, none), jnp.where(m, none, rows32)], axis=0)
                hi, lo = split(both)
                unfolded[p, i] = jnp.concatenate([hi, lo], axis=1)

    def first_half(h):
        def step(k, carry):
            i = 4 * h + k
            hop_send[h, :, lanes(k)] = (acc[:, lanes(i)] + far_rows(2, i)).astype(BF16)
            return carry

        lax.fori_loop(0, 4, step, 0, unroll=4)
        to = ys[0] if h == 0 else ys[2]
        return remote(hop_send.at[h], hop_recv.at[h], s_send.at[2, h], s_recv.at[2, h], {"near": to})

    def middle_half(h):
        def step(k, carry):
            i = 4 * h + k
            near = near_rows((0, 1), i)
            passed = hop_recv[h, :, lanes(k)].astype(F32)
            for p in range(2):
                total = near[64 * p : 64 * p + 64] + far_rows(p, i)
                if p == h:
                    total = total + passed
                send_buf[p, h, :, lanes(k)] = total.astype(BF16)
            return carry

        lax.fori_loop(0, 4, step, 0, unroll=4)
        return [
            remote(send_buf.at[p, h], recv_buf.at[p, h], s_send.at[p, h], s_recv.at[p, h], {"near": ys[2 * p]})
            for p in range(2)
        ]

    def last_half(h):
        def step(k, carry):
            i = 4 * h + k
            acc[:, lanes(i)] = near_rows((3,), i) + far_rows(3, i)
            return carry

        lax.fori_loop(0, 4, step, 0, unroll=4)

    for c in x_copies:
        c.wait_recv()
    plane = pl.ds(z * 4, 4)
    z_copies = [
        remote(gbuf.at[plane], gbuf.at[plane], z_send.at[d], z_recv.at[d], {"leaf": zs[d]}) for d in range(7)
    ]

    outer_halos[0] = halo(0, outer, outer_side, 0)

    for c in y_copies:
        c.wait_recv()
    ucp_copy = remote(
        ucp.at[pl.ds(1, 3), some], ucp.at[pl.ds(1, 3), some], ucp_sem.at[0], ucp_sem.at[1], {"leaf": mate}
    )

    def arrive(p):
        outer_halos[p].wait_recv()
        mate_halos[p].wait_recv()

    arrive(2)
    outer_halos[1] = halo(1, outer, outer_side, 0)
    for c in get_nb:
        c.wait()

    def near_step(i, carry):
        acc[:, lanes(i)] = near_rows((2,), i)
        return carry

    lax.fori_loop(0, 8, near_step, 0, unroll=4)
    mate_coefs.wait_recv()
    for c in shares:
        c.wait_recv()
    get_lc.wait()
    local_fields()
    descend(0, 96, None)
    hops = [first_half(0), first_half(1)]

    arrive(0)
    outer_halos[3] = halo(3, outer, outer_side, 0)

    for c in z_copies:
        c.wait_recv()
    for m in range(2, 7):
        for p in range(64 >> m):
            if m == 2:
                pair = [gbuf[2 * p], gbuf[2 * p + 1]]
            else:
                c0 = OFF[m - 1] - 32 + 2 * p
                pair = [ups[c0], ups[c0 + 1]]
            row = OFF[m] - 32 + p
            ups[row] = nt(jnp.concatenate(pair, axis=1), bdu[row]).astype(BF16)
    ucp_copy.wait_recv()
    for c in i_copies:
        c.wait_recv()
    down = None
    for m in range(6, 0, -1):
        f = None
        for d in range(4):
            got = []
            for t in range(2):
                q = within(ints[d, t, ancestors[m]], 64 >> m)
                got.append(gbuf[q] if m == 1 else ups[OFF[m] - 32 + q])
            part = nt(jnp.concatenate(got, axis=1), paired(ucp[d, m - 1]))
            f = part if f is None else f + part
        if down is not None:
            f = f + down
        both = lowered(f, bd1 if m == 1 else bdu[ancestors[m] - 32])
        even = lax.rem(l // (1 << (m - 1)), 2) == 0
        down = jnp.where(even, both[:, 0:128], both[:, 128:256])
        if m == 1:
            down_send[...] = jnp.where(even, both[:, 128:256], both[:, 0:128])
            downs[core] = down
    down_copy = remote(down_send, downs.at[core], down_sem.at[0], down_sem.at[1], {"leaf": mate})


    arrive(1)
    hops[0].wait_recv()
    sums = middle_half(0)
    hops[1].wait_recv()
    sums += middle_half(1)

    down_copy.wait_recv()
    descend(96, 128, jnp.concatenate([downs[0], downs[1]], axis=0))
    arrive(3)
    last_half(0)
    last_half(1)
    for c in sums:
        c.wait_recv()
    for h in range(2):
        at = pl.ds(1024 * h, 1024)
        out[:, at] = (
            acc[:, at] + recv_buf[0, h].astype(F32) + recv_buf[1, h].astype(F32)
        ).astype(BF16)
    for c in sends:
        c.wait_send()


def local(
    vectors,
    near_blocks,
    near_cols,
    near_count,
    col_basis,
    row_basis,
    local_transfer,
    local_coupling,
    local_partners,
    upper_transfer,
    upper_coupling,
    upper_partners,
):
    anywhere = pl.BlockSpec(memory_space=pl.ANY)
    scalars = pl.BlockSpec(memory_space=pltpu.SMEM)
    dma = pltpu.SemaphoreType.DMA
    vm = pltpu.VMEM
    return pl.pallas_call(
        kernel,
        out_shape=jax.ShapeDtypeStruct((64, 2048), BF16),
        in_specs=[
            anywhere,
            anywhere,
            scalars,
            scalars,
            anywhere,
            anywhere,
            anywhere,
            anywhere,
            scalars,
            anywhere,
            anywhere,
            anywhere,
        ],
        out_specs=pl.BlockSpec(memory_space=pltpu.VMEM),
        scratch_shapes=[vm((24, 64, 256), BF16) for _ in range(4)]
        + [
            vm((8, 8, 256, 256), BF16),
            vm((64, 2048), BF16),
            vm((64, 2048), BF16),
            vm((8, 256, 256), BF16),
            vm((7, 64, 128), BF16),
            vm((15, 64, 128), BF16),
            vm((31, 64, 128), BF16),
            vm((64, 128), BF16),
            vm((4, 6, 64, 128), BF16),
            pltpu.SMEM((4, 2, 63), jnp.int32),
            vm((3, 15, 128, 128), BF16),
            vm((15, 128, 128), F32),
            vm((7, 128, 256), BF16),
            vm((31, 128, 256), BF16),
            vm((4, 8, 64, 256), BF16),
            vm((2, 16, 128), BF16),
            vm((32, 16, 128), BF16),
            vm((31, 16, 128), BF16),
            vm((16, 128), F32),
            vm((2, 16, 128), F32),
            vm((2, 64, 1024), BF16),
            vm((2, 64, 1024), BF16),
            vm((2, 2, 64, 1024), BF16),
            vm((2, 2, 64, 1024), BF16),
            vm((64, 2048), F32),
            dma((11,)),
            dma((4, 8)),
            dma((8,)),
            dma((6,)),
            dma((4, 2)),
            dma((4, 2)),
            dma((2,)),
            dma((2,)),
            dma((3,)),
            dma((3,)),
            dma((3,)),
            dma((3,)),
            dma((2,)),
            dma((2,)),
            dma((2,)),
            dma((2,)),
            dma((2,)),
            dma((3,)),
            dma((3,)),
            dma((7,)),
            dma((7,)),
            dma((3, 2)),
            dma((3, 2)),
        ],
        compiler_params=pltpu.CompilerParams(
            collective_id=0, has_side_effects=True, vmem_limit_bytes=63 * 1024 * 1024
        ),
        name="h2",
    )(
        vectors,
        near_blocks,
        near_cols,
        near_count,
        col_basis,
        row_basis,
        local_transfer,
        local_coupling,
        local_partners.T,
        upper_transfer,
        upper_coupling,
        upper_partners.T,
    )


def solution(mesh):
    return jax.shard_map(
        local,
        mesh=mesh,
        in_specs=(
            P(None, "leaf"),
            P("leaf", "near", None, None),
            P("leaf", "near"),
            P("leaf"),
            P(None, "leaf"),
            P(None, "leaf"),
            P("leaf", None, None),
            P("leaf", None, "near"),
            P("leaf", "near"),
            P(),
            P(None, None, "near"),
            P(None, "near"),
        ),
        out_specs=P("near", "leaf"),
        check_vma=False,
    )
```

```python
import functools

import jax
import jax.numpy as jnp
from jax import lax
from jax.experimental import pallas as pl
from jax.experimental.pallas import tpu as pltpu
from jax.sharding import PartitionSpec as P

F32, BF16 = jnp.float32, jnp.bfloat16
MESH = pl.DeviceIdType.MESH
ORDER = (1, 3, 2, 0)
START = (0, 8, 12, 14)
OFF = (None, 0, 32, 48, 56, 60, 62)


def nt(a, b):
    return lax.dot_general(a, b, (((1,), (1,)), ((), ())), preferred_element_type=F32)


def nn(a, b):
    return lax.dot_general(a, b, (((1,), (0,)), ((), ())), preferred_element_type=F32)


def within(index, size):
    return jnp.minimum(jnp.maximum(index, 0), size - 1)


def low_half(shape):
    return lax.broadcasted_iota(jnp.int32, shape, 1) < 64


def paired(t):
    t = t.astype(F32)
    r = pltpu.roll(t, 64, 1)
    m = low_half(t.shape)
    z = jnp.zeros_like(t)
    top = jnp.concatenate([jnp.where(m, t, z), jnp.where(m, r, z)], axis=1)
    low = jnp.concatenate([jnp.where(m, z, r), jnp.where(m, z, t)], axis=1)
    return jnp.concatenate([top, low], axis=0).astype(BF16)


def split(f):
    hi = f.astype(BF16)
    lo = (f - hi.astype(F32)).astype(BF16)
    return hi, lo


def lowered(f, bd):
    hi, lo = split(f)
    return nn(jnp.concatenate([hi, lo], axis=1), jnp.concatenate([bd, bd], axis=0))


def kernel(
    vectors,
    near_blocks,
    near_cols,
    near_count,
    col_basis,
    row_basis,
    local_transfer,
    local_coupling,
    local_partners,
    upper_transfer,
    upper_coupling,
    upper_partners,
    out,
    wide0,
    wide1,
    wide2,
    wide3,
    nb,
    cb,
    rb,
    rb4,
    lt,
    lc,
    ut,
    ut1,
    ucp,
    ints,
    win,
    field,
    bdt,
    bdu,
    unfolded,
    rootpair,
    gbuf,
    ups,
    down_send,
    downs,
    hop_send,
    hop_recv,
    send_buf,
    recv_buf,
    acc,
    held,
    loc_sem,
    own_sem,
    nb_sem,
    anc_sem,
    halo_send,
    halo_recv,
    coef_send,
    coef_recv,
    y_send,
    y_recv,
    i_send,
    i_recv,
    share_send,
    share_recv,
    mate_sem,
    down_sem,
    ucp_sem,
    x_send,
    x_recv,
    z_send,
    z_recv,
    s_send,
    s_recv,
):
    l = lax.axis_index("leaf")
    y = lax.axis_index("near")
    core = lax.rem(l, 2)
    outer = lax.rem(l + 63 + 2 * core, 64)
    outer_side = 2 - 2 * core
    mate_side = 2 * core
    inside = jnp.logical_and(l > 0, l < 63)
    chip = l // 2
    x = lax.rem(chip, 4)
    z = chip // 4
    mate = l + 1 - 2 * core
    wides = (wide0, wide1, wide2, wide3)
    xs = [(z * 4 + lax.rem(x + d, 4)) * 2 + core for d in range(1, 4)]
    zs = [(lax.rem(z + d, 8) * 4 + x) * 2 + core for d in range(1, 8)]
    ys = [lax.rem(y + d, 4) for d in range(1, 4)]
    rows = [pl.multiple_of(lax.rem(y + d, 4) * 64, 64) for d in ORDER]
    ancestors = [None] + [OFF[m] + l // (1 << m) for m in range(1, 7)]

    barrier = pltpu.get_barrier_semaphore()
    for t in [outer, mate] + xs + zs:
        pl.semaphore_signal(barrier, inc=1, device_id={"leaf": t}, device_id_type=MESH)
    for t in ys:
        pl.semaphore_signal(barrier, inc=1, device_id={"near": t}, device_id_type=MESH)

    def here(src, dst, sem):
        c = pltpu.make_async_copy(src, dst, sem)
        c.start()
        return c

    get_cb = here(col_basis, cb, loc_sem.at[4])
    get_lt = here(local_transfer, lt, loc_sem.at[5])
    own = [
        [
            here(
                vectors.at[pl.ds(rows[p], 64), pl.ds(256 * i, 256)],
                wides[p].at[8 + i],
                own_sem.at[p, i],
            )
            for i in range(8)
        ]
        for p in range(4)
    ]
    get_anc = [
        here(upper_coupling.at[ancestors[m]], ucp.at[0, m - 1], anc_sem.at[m - 1])
        for m in range(1, 7)
    ]
    get_ints = here(upper_partners, ints.at[0], loc_sem.at[6])
    get_ut1 = here(upper_transfer.at[chip], ut1, loc_sem.at[7])

    sends = []

    def remote(src, dst, s, r, target):
        c = pltpu.make_async_remote_copy(
            src_ref=src, dst_ref=dst, send_sem=s, recv_sem=r, device_id=target, device_id_type=MESH
        )
        c.start()
        sends.append(c)
        return c

    class Outer:
        def __init__(self, *args):
            src, dst, s, r = args
            self.copy = pltpu.make_async_remote_copy(
                src_ref=src, dst_ref=dst, send_sem=s, recv_sem=r, device_id={"leaf": outer}, device_id_type=MESH
            )
            pl.when(inside)(self.copy.start)
            sends.append(self)

        def wait_recv(self):
            pl.when(inside)(self.copy.wait_recv)

        def wait_send(self):
            pl.when(inside)(self.copy.wait_send)

    def outer_halo(p):
        src = wides[p].at[pl.ds(8, 8)]
        return Outer(src, wides[p].at[pl.ds(8 * outer_side, 8)], halo_send.at[p, 0], halo_recv.at[p, 0])

    def halo(p, to, side, k):
        return remote(
            wides[p].at[pl.ds(8, 8)], wides[p].at[pl.ds(8 * side, 8)], halo_send.at[p, k], halo_recv.at[p, k], {"leaf": to}
        )

    get_lt.wait()
    for p in range(7):
        bdt[p] = paired(lt[p])
    for p in range(4):
        for c in own[p]:
            c.wait()
    get_cb.wait()
    for i in range(8):
        w = cb[:, 256 * i : 256 * (i + 1)]
        none = jnp.zeros_like(w)
        first = jnp.concatenate([wides[p][8 + i, 0:32, :] for p in range(4)], axis=0)
        second = jnp.concatenate([wides[p][8 + i, 32:64, :] for p in range(4)], axis=0)
        f = nt(first, jnp.concatenate([w, none], axis=0)) + nt(second, jnp.concatenate([none, w], axis=0))
        win[1, i] = f.astype(BF16)
    for level in range(3):
        for g in range(4 >> level):
            c0 = START[level] + 2 * g
            pair = jnp.concatenate([win[1, c0], win[1, c0 + 1]], axis=1)
            win[1, START[level + 1] + g] = nt(pair, bdt[START[level + 1] - 8 + g]).astype(BF16)
    get_lc = here(local_coupling, lc, loc_sem.at[8])
    get_ut = here(upper_transfer.at[pl.ds(32, 31)], ut, loc_sem.at[9])
    get_rb = here(row_basis, rb, loc_sem.at[10])
    get_nb = [here(near_blocks.at[i], nb.at[i], nb_sem.at[i]) for i in range(8)]
    mine = pl.ds(pl.multiple_of(96 + 16 * core, 16), 16)
    other = pl.ds(pl.multiple_of(112 - 16 * core, 16), 16)
    rootpair[core] = win[1, 14, mine, :]
    for c in get_anc:
        c.wait()
    get_ints.wait()

    pl.semaphore_wait(barrier, 2 + 3 + 7 + 3)
    mate_copy = remote(
        win.at[1, 14, other], rootpair.at[core], mate_sem.at[0], mate_sem.at[1], {"leaf": mate}
    )
    outer_coefs = Outer(
        win.at[1, :, pl.ds(64, 64)], win.at[outer_side, :, pl.ds(64, 64)], coef_send.at[0], coef_recv.at[0]
    )
    y_copies, i_copies = [], []
    some = pl.ds(3 * core, 3)
    for d in range(1, 4):
        to = {"near": ys[d - 1]}
        y_copies.append(remote(ucp.at[0, some], ucp.at[d, some], y_send.at[d - 1], y_recv.at[d - 1], to))
        i_copies.append(remote(upper_partners, ints.at[d], i_send.at[d - 1], i_recv.at[d - 1], to))
    outer_halos = {}
    mate_coefs = remote(win.at[1], win.at[mate_side], coef_send.at[1], coef_recv.at[1], {"leaf": mate})
    mate_halos = [halo(p, mate, mate_side, 1) for p in range(4)]

    get_ut1.wait()
    bd1 = paired(ut1[...])
    mate_copy.wait_recv()
    gbuf[x, z] = nt(jnp.concatenate([rootpair[0], rootpair[1]], axis=1), bd1).astype(BF16)
    z_copies = [
        remote(gbuf.at[x, z], gbuf.at[x, z], z_send.at[d], z_recv.at[d], {"leaf": zs[d]}) for d in range(7)
    ]
    outer_halos[2] = outer_halo(2)
    outer_coefs.wait_recv()
    got = 2 * core
    shares = [
        remote(
            win.at[got, :, pl.ds(96, 32)],
            win.at[got, :, pl.ds(32 * p, 32)],
            share_send.at[p],
            share_recv.at[p],
            {"near": ys[3 - ORDER[p]]},
        )
        for p in range(2)
    ]

    get_rb.wait()
    for i in range(8):
        w = rb[:, 256 * i : 256 * (i + 1)]
        rb4[i] = jnp.concatenate([w, w, w, w], axis=0)
    get_ut.wait()
    for p in range(31):
        bdu[p] = paired(ut[p])

    def near_rows(chunks, i):
        total = jnp.zeros((64 * len(chunks), 256), F32)
        for t in range(8):
            j = within(near_cols[i, t] - (l - 1) * 8, 24)
            taken = jnp.concatenate([wides[p][j] for p in chunks], axis=0)
            live = jnp.full(taken.shape, near_count[i], jnp.int32) > y * 8 + t
            taken = jnp.where(live, taken, jnp.zeros_like(taken))
            total = total + nn(taken, nb[i, t])
        return total

    def far_rows(p, i):
        return nn(unfolded[p, i], rb4[i])

    def lanes(i):
        return pl.ds(pl.multiple_of(i * 256, 256), 256)

    def local_fields():
        for level in range(4):
            count = 8 >> level
            for g in range(count):
                q = START[level] + g
                got = []
                for t in range(2):
                    w = within(local_partners[t, q] - (l - 1) * count, 3 * count)
                    side = lax.shift_right_logical(w, 3 - level)
                    got.append(win[side, START[level] + w - side * count])
                field[q] = nt(jnp.concatenate(got, axis=1), paired(lc[q]))

    def descend(begin, end, extra):
        top = field[14, begin:end, :]
        downs = [top if extra is None else top + extra]
        for level in (2, 1, 0):
            lower = []
            for g, f in enumerate(downs):
                both = lowered(f, bdt[START[level + 1] - 8 + g])
                q = START[level] + 2 * g
                lower.append(both[:, 0:128] + field[q, begin:end, :])
                lower.append(both[:, 128:256] + field[q + 1, begin:end, :])
            downs = lower
        for i, f in enumerate(downs):
            for p in range(begin // 32, end // 32):
                rows32 = f[32 * p - begin : 32 * p - begin + 32, :]
                none = jnp.zeros_like(rows32)
                m = low_half((32, 128))
                both = jnp.concatenate([jnp.where(m, rows32, none), jnp.where(m, none, rows32)], axis=0)
                hi, lo = split(both)
                unfolded[p, i] = jnp.concatenate([hi, lo], axis=1)

    def first_half(h):
        def step(k, carry):
            i = 4 * h + k
            hop_send[h, :, lanes(k)] = (acc[:, lanes(i)] + far_rows(2, i)).astype(BF16)
            return carry

        lax.fori_loop(0, 4, step, 0, unroll=4)
        to = ys[0] if h == 0 else ys[2]
        return remote(hop_send.at[h], hop_recv.at[h], s_send.at[2, h], s_recv.at[2, h], {"near": to})

    def middle(p, h, near, passed):
        def step(k, carry):
            i = 4 * h + k
            total = (near_rows((p,), i) if near else held[:, lanes(k)]) + far_rows(p, i)
            if passed:
                total = total + hop_recv[h, :, lanes(k)].astype(F32)
            send_buf[p, h, :, lanes(k)] = total.astype(BF16)
            return carry

        lax.fori_loop(0, 4, step, 0, unroll=4)
        return remote(
            send_buf.at[p, h], recv_buf.at[p, h], s_send.at[p, h], s_recv.at[p, h], {"near": ys[2 * p]}
        )

    for c in z_copies:
        c.wait_recv()
    x_copies = [
        remote(gbuf.at[x], gbuf.at[x], x_send.at[d], x_recv.at[d], {"leaf": xs[d]}) for d in range(3)
    ]

    outer_halos[0] = outer_halo(0)

    def arrive(p):
        outer_halos[p].wait_recv()
        mate_halos[p].wait_recv()

    arrive(2)
    outer_halos[1] = outer_halo(1)
    for c in get_nb:
        c.wait()

    def near_step(i, carry):
        acc[:, lanes(i)] = near_rows((2,), i)
        return carry

    lax.fori_loop(0, 8, near_step, 0, unroll=4)
    for c in y_copies:
        c.wait_recv()
    ucp_copy = remote(
        ucp.at[pl.ds(1, 3), some], ucp.at[pl.ds(1, 3), some], ucp_sem.at[0], ucp_sem.at[1], {"leaf": mate}
    )

    mate_coefs.wait_recv()
    for c in shares:
        c.wait_recv()
    get_lc.wait()
    local_fields()
    descend(0, 96, None)
    hops = [first_half(0), first_half(1)]

    arrive(0)
    outer_halos[3] = outer_halo(3)

    sums = [middle(0, 1, True, False)]

    def held_step(k, carry):
        held[:, lanes(k)] = near_rows((0,), k)
        return carry

    lax.fori_loop(0, 4, held_step, 0, unroll=4)
    arrive(1)
    sums.append(middle(1, 0, True, False))
    hops[0].wait_recv()
    sums.append(middle(0, 0, False, True))
    hops[1].wait_recv()
    sums.append(middle(1, 1, True, True))

    for c in x_copies:
        c.wait_recv()
    for m in range(2, 7):
        for p in range(64 >> m):
            if m == 2:
                pair = [gbuf[2 * p % 4, p // 2], gbuf[2 * p % 4 + 1, p // 2]]
            else:
                c0 = OFF[m - 1] - 32 + 2 * p
                pair = [ups[c0], ups[c0 + 1]]
            row = OFF[m] - 32 + p
            ups[row] = nt(jnp.concatenate(pair, axis=1), bdu[row]).astype(BF16)
    ucp_copy.wait_recv()
    for c in i_copies:
        c.wait_recv()
    down = None
    for m in range(6, 0, -1):
        f = None
        for d in range(4):
            got = []
            for t in range(2):
                q = within(ints[d, t, ancestors[m]], 64 >> m)
                if m == 1:
                    got.append(gbuf[lax.bitwise_and(q, 3), lax.shift_right_logical(q, 2)])
                else:
                    got.append(ups[OFF[m] - 32 + q])
            part = nt(jnp.concatenate(got, axis=1), paired(ucp[d, m - 1]))
            f = part if f is None else f + part
        if down is not None:
            f = f + down
        both = lowered(f, bd1 if m == 1 else bdu[ancestors[m] - 32])
        even = lax.rem(l // (1 << (m - 1)), 2) == 0
        down = jnp.where(even, both[:, 0:128], both[:, 128:256])
        if m == 1:
            down_send[...] = jnp.where(even, both[:, 128:256], both[:, 0:128])
            downs[core] = down
    down_copy = remote(down_send, downs.at[core], down_sem.at[0], down_sem.at[1], {"leaf": mate})


    arrive(3)

    def own_step(i, carry):
        acc[:, lanes(i)] = near_rows((3,), i)
        return carry

    lax.fori_loop(0, 8, own_step, 0, unroll=4)
    down_copy.wait_recv()
    descend(96, 128, jnp.concatenate([downs[0], downs[1]], axis=0))
    for c in sums:
        c.wait_recv()
    for h in range(2):

        def final_step(k, carry):
            i = 4 * h + k
            total = acc[:, lanes(i)] + far_rows(3, i)
            total = total + recv_buf[0, h, :, lanes(k)].astype(F32) + recv_buf[1, h, :, lanes(k)].astype(F32)
            out[:, lanes(i)] = total.astype(BF16)
            return carry

        lax.fori_loop(0, 4, final_step, 0, unroll=4)
    for c in sends:
        c.wait_send()


def local(
    vectors,
    near_blocks,
    near_cols,
    near_count,
    col_basis,
    row_basis,
    local_transfer,
    local_coupling,
    local_partners,
    upper_transfer,
    upper_coupling,
    upper_partners,
):
    anywhere = pl.BlockSpec(memory_space=pl.ANY)
    scalars = pl.BlockSpec(memory_space=pltpu.SMEM)
    dma = pltpu.SemaphoreType.DMA
    vm = pltpu.VMEM
    return pl.pallas_call(
        kernel,
        out_shape=jax.ShapeDtypeStruct((64, 2048), BF16),
        in_specs=[
            anywhere,
            anywhere,
            scalars,
            scalars,
            anywhere,
            anywhere,
            anywhere,
            anywhere,
            scalars,
            anywhere,
            anywhere,
            anywhere,
        ],
        out_specs=pl.BlockSpec(memory_space=pltpu.VMEM),
        scratch_shapes=[vm((24, 64, 256), BF16) for _ in range(4)]
        + [
            vm((8, 8, 256, 256), BF16),
            vm((64, 2048), BF16),
            vm((64, 2048), BF16),
            vm((8, 256, 256), BF16),
            vm((7, 64, 128), BF16),
            vm((15, 64, 128), BF16),
            vm((31, 64, 128), BF16),
            vm((64, 128), BF16),
            vm((4, 6, 64, 128), BF16),
            pltpu.SMEM((4, 2, 63), jnp.int32),
            vm((3, 15, 128, 128), BF16),
            vm((15, 128, 128), F32),
            vm((7, 128, 256), BF16),
            vm((31, 128, 256), BF16),
            vm((4, 8, 64, 256), BF16),
            vm((2, 16, 128), BF16),
            vm((4, 8, 16, 128), BF16),
            vm((31, 16, 128), BF16),
            vm((16, 128), F32),
            vm((2, 16, 128), F32),
            vm((2, 64, 1024), BF16),
            vm((2, 64, 1024), BF16),
            vm((2, 2, 64, 1024), BF16),
            vm((2, 2, 64, 1024), BF16),
            vm((64, 2048), F32),
            vm((64, 1024), F32),
            dma((11,)),
            dma((4, 8)),
            dma((8,)),
            dma((6,)),
            dma((4, 2)),
            dma((4, 2)),
            dma((2,)),
            dma((2,)),
            dma((3,)),
            dma((3,)),
            dma((3,)),
            dma((3,)),
            dma((2,)),
            dma((2,)),
            dma((2,)),
            dma((2,)),
            dma((2,)),
            dma((3,)),
            dma((3,)),
            dma((7,)),
            dma((7,)),
            dma((3, 2)),
            dma((3, 2)),
        ],
        compiler_params=pltpu.CompilerParams(
            collective_id=0, has_side_effects=True, vmem_limit_bytes=63 * 1024 * 1024
        ),
        name="h2",
    )(
        vectors,
        near_blocks,
        near_cols,
        near_count,
        col_basis,
        row_basis,
        local_transfer,
        local_coupling,
        local_partners.T,
        upper_transfer,
        upper_coupling,
        upper_partners.T,
    )


def solution(mesh):
    return jax.shard_map(
        local,
        mesh=mesh,
        in_specs=(
            P(None, "leaf"),
            P("leaf", "near", None, None),
            P("leaf", "near"),
            P("leaf"),
            P(None, "leaf"),
            P(None, "leaf"),
            P("leaf", None, None),
            P("leaf", None, "near"),
            P("leaf", "near"),
            P(),
            P(None, None, "near"),
            P(None, "near"),
        ),
        out_specs=P("near", "leaf"),
        check_vma=False,
    )
```

```python
import functools

import jax
import jax.numpy as jnp
from jax import lax
from jax.experimental import pallas as pl
from jax.experimental.pallas import tpu as pltpu
from jax.sharding import PartitionSpec as P

F32, BF16 = jnp.float32, jnp.bfloat16
MESH = pl.DeviceIdType.MESH
ORDER = (1, 3, 2, 0)
START = (0, 8, 12, 14)
OFF = (None, 0, 32, 48, 56, 60, 62)


def nt(a, b):
    return lax.dot_general(a, b, (((1,), (1,)), ((), ())), preferred_element_type=F32)


def nn(a, b):
    return lax.dot_general(a, b, (((1,), (0,)), ((), ())), preferred_element_type=F32)


def within(index, size):
    return jnp.minimum(jnp.maximum(index, 0), size - 1)


def low_half(shape):
    return lax.broadcasted_iota(jnp.int32, shape, 1) < 64


def paired(t):
    t = t.astype(F32)
    r = pltpu.roll(t, 64, 1)
    m = low_half(t.shape)
    z = jnp.zeros_like(t)
    top = jnp.concatenate([jnp.where(m, t, z), jnp.where(m, r, z)], axis=1)
    low = jnp.concatenate([jnp.where(m, z, r), jnp.where(m, z, t)], axis=1)
    return jnp.concatenate([top, low], axis=0).astype(BF16)


def split(f):
    hi = f.astype(BF16)
    lo = (f - hi.astype(F32)).astype(BF16)
    return hi, lo


def lowered(f, bd):
    hi, lo = split(f)
    return nn(jnp.concatenate([hi, lo], axis=1), jnp.concatenate([bd, bd], axis=0))


def kernel(
    vectors,
    near_blocks,
    near_cols,
    near_count,
    col_basis,
    row_basis,
    local_transfer,
    local_coupling,
    local_partners,
    upper_transfer,
    upper_coupling,
    upper_partners,
    out,
    wide0,
    wide1,
    wide2,
    wide3,
    nb,
    cb,
    rb,
    rb4,
    lt,
    lc,
    ut,
    ut1,
    ucp,
    ints,
    win,
    field,
    bdt,
    bdu,
    unfolded,
    rootpair,
    gbuf,
    ups,
    down_send,
    downs,
    hop_send,
    hop_recv,
    send_buf,
    recv_buf,
    acc,
    held,
    loc_sem,
    own_sem,
    nb_sem,
    anc_sem,
    halo_send,
    halo_recv,
    coef_send,
    coef_recv,
    y_send,
    y_recv,
    i_send,
    i_recv,
    share_send,
    share_recv,
    mate_sem,
    down_sem,
    ucp_sem,
    x_send,
    x_recv,
    z_send,
    z_recv,
    s_send,
    s_recv,
):
    l = lax.axis_index("leaf")
    y = lax.axis_index("near")
    core = lax.rem(l, 2)
    outer = lax.rem(l + 63 + 2 * core, 64)
    outer_side = 2 - 2 * core
    mate_side = 2 * core
    inside = jnp.logical_and(l > 0, l < 63)
    chip = l // 2
    x = lax.rem(chip, 4)
    z = chip // 4
    mate = l + 1 - 2 * core
    wides = (wide0, wide1, wide2, wide3)
    xs = [(z * 4 + lax.rem(x + d, 4)) * 2 + core for d in range(1, 4)]
    zs = [(lax.rem(z + d, 8) * 4 + x) * 2 + core for d in range(1, 8)]
    ys = [lax.rem(y + d, 4) for d in range(1, 4)]
    rows = [pl.multiple_of(lax.rem(y + d, 4) * 64, 64) for d in ORDER]
    ancestors = [None] + [OFF[m] + l // (1 << m) for m in range(1, 7)]

    barrier = pltpu.get_barrier_semaphore()
    for t in zs + xs + [outer, mate]:
        pl.semaphore_signal(barrier, inc=1, device_id={"leaf": t}, device_id_type=MESH)
    for t in ys:
        pl.semaphore_signal(barrier, inc=1, device_id={"near": t}, device_id_type=MESH)

    def here(src, dst, sem):
        c = pltpu.make_async_copy(src, dst, sem)
        c.start()
        return c

    get_cb = here(col_basis, cb, loc_sem.at[4])
    get_lt = here(local_transfer, lt, loc_sem.at[5])
    own = [
        [
            here(
                vectors.at[pl.ds(rows[p], 64), pl.ds(256 * i, 256)],
                wides[p].at[8 + i],
                own_sem.at[p, i],
            )
            for i in range(8)
        ]
        for p in range(4)
    ]
    get_anc = [
        here(upper_coupling.at[ancestors[m]], ucp.at[0, m - 1], anc_sem.at[m - 1])
        for m in range(1, 7)
    ]
    get_ints = here(upper_partners, ints.at[0], loc_sem.at[6])
    get_ut1 = here(upper_transfer.at[chip], ut1, loc_sem.at[7])

    sends = []

    def remote(src, dst, s, r, target):
        c = pltpu.make_async_remote_copy(
            src_ref=src, dst_ref=dst, send_sem=s, recv_sem=r, device_id=target, device_id_type=MESH
        )
        c.start()
        sends.append(c)
        return c

    class Outer:
        def __init__(self, *args):
            src, dst, s, r = args
            self.copy = pltpu.make_async_remote_copy(
                src_ref=src, dst_ref=dst, send_sem=s, recv_sem=r, device_id={"leaf": outer}, device_id_type=MESH
            )
            pl.when(inside)(self.copy.start)
            sends.append(self)

        def wait_recv(self):
            pl.when(inside)(self.copy.wait_recv)

        def wait_send(self):
            pl.when(inside)(self.copy.wait_send)

    def outer_halo(p):
        src = wides[p].at[pl.ds(8, 8)]
        return Outer(src, wides[p].at[pl.ds(8 * outer_side, 8)], halo_send.at[p, 0], halo_recv.at[p, 0])

    def halo(p, to, side, k):
        return remote(
            wides[p].at[pl.ds(8, 8)], wides[p].at[pl.ds(8 * side, 8)], halo_send.at[p, k], halo_recv.at[p, k], {"leaf": to}
        )

    get_lt.wait()
    for p in range(7):
        bdt[p] = paired(lt[p])
    for p in range(4):
        for c in own[p]:
            c.wait()
    get_cb.wait()
    for i in range(8):
        w = cb[:, 256 * i : 256 * (i + 1)]
        none = jnp.zeros_like(w)
        first = jnp.concatenate([wides[p][8 + i, 0:32, :] for p in range(4)], axis=0)
        second = jnp.concatenate([wides[p][8 + i, 32:64, :] for p in range(4)], axis=0)
        f = nt(first, jnp.concatenate([w, none], axis=0)) + nt(second, jnp.concatenate([none, w], axis=0))
        win[1, i] = f.astype(BF16)
    for level in range(3):
        for g in range(4 >> level):
            c0 = START[level] + 2 * g
            pair = jnp.concatenate([win[1, c0], win[1, c0 + 1]], axis=1)
            win[1, START[level + 1] + g] = nt(pair, bdt[START[level + 1] - 8 + g]).astype(BF16)
    get_lc = here(local_coupling, lc, loc_sem.at[8])
    get_ut = here(upper_transfer.at[pl.ds(32, 31)], ut, loc_sem.at[9])
    get_rb = here(row_basis, rb, loc_sem.at[10])
    get_nb = [here(near_blocks.at[i], nb.at[i], nb_sem.at[i]) for i in range(8)]
    mine = pl.ds(pl.multiple_of(96 + 16 * core, 16), 16)
    other = pl.ds(pl.multiple_of(112 - 16 * core, 16), 16)
    rootpair[core] = win[1, 14, mine, :]
    for c in get_anc:
        c.wait()
    get_ints.wait()

    pl.semaphore_wait(barrier, 2 + 3 + 7 + 3)
    mate_copy = remote(
        win.at[1, 14, other], rootpair.at[core], mate_sem.at[0], mate_sem.at[1], {"leaf": mate}
    )
    outer_coefs = [
        Outer(
            win.at[1, :, pl.ds(begin, 32)], win.at[outer_side, :, pl.ds(begin, 32)], coef_send.at[k], coef_recv.at[k]
        )
        for k, begin in ((0, 96), (2, 64))
    ]
    outer_halos = {}
    mate_coefs = remote(win.at[1], win.at[mate_side], coef_send.at[1], coef_recv.at[1], {"leaf": mate})
    mate_halos = [halo(p, mate, mate_side, 1) for p in range(4)]

    get_ut1.wait()
    bd1 = paired(ut1[...])
    mate_copy.wait_recv()
    gbuf[x, z] = nt(jnp.concatenate([rootpair[0], rootpair[1]], axis=1), bd1).astype(BF16)
    z_copies = [
        remote(gbuf.at[x, z], gbuf.at[x, z], z_send.at[d], z_recv.at[d], {"leaf": zs[d]}) for d in range(7)
    ]
    outer_halos[2] = outer_halo(2)
    outer_halos[0] = outer_halo(0)
    outer_coefs[0].wait_recv()
    got = 2 * core
    shares = [
        remote(
            win.at[got, :, pl.ds(96, 32)],
            win.at[got, :, pl.ds(32 * p, 32)],
            share_send.at[p],
            share_recv.at[p],
            {"near": ys[3 - ORDER[p]]},
        )
        for p in range(2)
    ]

    y_copies, i_copies = [], []
    some = pl.ds(3 * core, 3)
    for d in range(1, 4):
        to = {"near": ys[d - 1]}
        y_copies.append(remote(ucp.at[0, some], ucp.at[d, some], y_send.at[d - 1], y_recv.at[d - 1], to))
        i_copies.append(remote(upper_partners, ints.at[d], i_send.at[d - 1], i_recv.at[d - 1], to))
    get_rb.wait()
    for i in range(8):
        w = rb[:, 256 * i : 256 * (i + 1)]
        rb4[i] = jnp.concatenate([w, w, w, w], axis=0)
    get_ut.wait()
    for p in range(31):
        bdu[p] = paired(ut[p])

    def near_rows(chunks, i):
        total = jnp.zeros((64 * len(chunks), 256), F32)
        for t in range(8):
            j = within(near_cols[i, t] - (l - 1) * 8, 24)
            taken = jnp.concatenate([wides[p][j] for p in chunks], axis=0)
            live = jnp.full(taken.shape, near_count[i], jnp.int32) > y * 8 + t
            taken = jnp.where(live, taken, jnp.zeros_like(taken))
            total = total + nn(taken, nb[i, t])
        return total

    def far_rows(p, i):
        return nn(unfolded[p, i], rb4[i])

    def lanes(i):
        return pl.ds(pl.multiple_of(i * 256, 256), 256)

    def local_fields():
        for level in range(4):
            count = 8 >> level
            for g in range(count):
                q = START[level] + g
                got = []
                for t in range(2):
                    w = within(local_partners[t, q] - (l - 1) * count, 3 * count)
                    side = lax.shift_right_logical(w, 3 - level)
                    got.append(win[side, START[level] + w - side * count])
                field[q] = nt(jnp.concatenate(got, axis=1), paired(lc[q]))

    def descend(begin, end, extra):
        top = field[14, begin:end, :]
        downs = [top if extra is None else top + extra]
        for level in (2, 1, 0):
            lower = []
            for g, f in enumerate(downs):
                both = lowered(f, bdt[START[level + 1] - 8 + g])
                q = START[level] + 2 * g
                lower.append(both[:, 0:128] + field[q, begin:end, :])
                lower.append(both[:, 128:256] + field[q + 1, begin:end, :])
            downs = lower
        for i, f in enumerate(downs):
            for p in range(begin // 32, end // 32):
                rows32 = f[32 * p - begin : 32 * p - begin + 32, :]
                none = jnp.zeros_like(rows32)
                m = low_half((32, 128))
                both = jnp.concatenate([jnp.where(m, rows32, none), jnp.where(m, none, rows32)], axis=0)
                hi, lo = split(both)
                unfolded[p, i] = jnp.concatenate([hi, lo], axis=1)

    def first_half(h):
        def step(k, carry):
            i = 4 * h + k
            hop_send[h, :, lanes(k)] = (acc[:, lanes(i)] + far_rows(2, i)).astype(BF16)
            return carry

        lax.fori_loop(0, 4, step, 0, unroll=4)
        to = ys[0] if h == 0 else ys[2]
        return remote(hop_send.at[h], hop_recv.at[h], s_send.at[2, h], s_recv.at[2, h], {"near": to})

    def middle(p, h, near, passed):
        def step(k, carry):
            i = 4 * h + k
            total = (near_rows((p,), i) if near else held[:, lanes(k)]) + far_rows(p, i)
            if passed:
                total = total + hop_recv[h, :, lanes(k)].astype(F32)
            send_buf[p, h, :, lanes(k)] = total.astype(BF16)
            return carry

        lax.fori_loop(0, 4, step, 0, unroll=4)
        return remote(
            send_buf.at[p, h], recv_buf.at[p, h], s_send.at[p, h], s_recv.at[p, h], {"near": ys[2 * p]}
        )


    def arrive(p):
        outer_halos[p].wait_recv()
        mate_halos[p].wait_recv()

    arrive(2)
    outer_halos[1] = outer_halo(1)
    for c in get_nb:
        c.wait()

    def near_step(i, carry):
        acc[:, lanes(i)] = near_rows((2,), i)
        return carry

    lax.fori_loop(0, 8, near_step, 0, unroll=4)
    for c in z_copies:
        c.wait_recv()
    x_copies = [
        remote(gbuf.at[x], gbuf.at[x], x_send.at[d], x_recv.at[d], {"leaf": xs[d]}) for d in range(3)
    ]

    mate_coefs.wait_recv()
    outer_coefs[1].wait_recv()
    for c in shares:
        c.wait_recv()
    get_lc.wait()
    local_fields()
    descend(0, 96, None)
    hops = [first_half(0), first_half(1)]
    for c in y_copies:
        c.wait_recv()
    ucp_copy = remote(
        ucp.at[pl.ds(1, 3), some], ucp.at[pl.ds(1, 3), some], ucp_sem.at[0], ucp_sem.at[1], {"leaf": mate}
    )


    arrive(0)
    outer_halos[3] = outer_halo(3)

    sums = [middle(0, 1, True, False)]

    def held_step(k, carry):
        held[:, lanes(k)] = near_rows((0,), k)
        return carry

    lax.fori_loop(0, 4, held_step, 0, unroll=4)
    arrive(1)
    sums.append(middle(1, 0, True, False))
    hops[0].wait_recv()
    sums.append(middle(0, 0, False, True))
    hops[1].wait_recv()
    sums.append(middle(1, 1, True, True))

    for c in x_copies:
        c.wait_recv()
    for m in range(2, 7):
        for p in range(64 >> m):
            if m == 2:
                pair = [gbuf[2 * p % 4, p // 2], gbuf[2 * p % 4 + 1, p // 2]]
            else:
                c0 = OFF[m - 1] - 32 + 2 * p
                pair = [ups[c0], ups[c0 + 1]]
            row = OFF[m] - 32 + p
            ups[row] = nt(jnp.concatenate(pair, axis=1), bdu[row]).astype(BF16)
    ucp_copy.wait_recv()
    for c in i_copies:
        c.wait_recv()
    down = None
    for m in range(6, 0, -1):
        f = None
        for d in range(4):
            got = []
            for t in range(2):
                q = within(ints[d, t, ancestors[m]], 64 >> m)
                if m == 1:
                    got.append(gbuf[lax.bitwise_and(q, 3), lax.shift_right_logical(q, 2)])
                else:
                    got.append(ups[OFF[m] - 32 + q])
            part = nt(jnp.concatenate(got, axis=1), paired(ucp[d, m - 1]))
            f = part if f is None else f + part
        if down is not None:
            f = f + down
        both = lowered(f, bd1 if m == 1 else bdu[ancestors[m] - 32])
        even = lax.rem(l // (1 << (m - 1)), 2) == 0
        down = jnp.where(even, both[:, 0:128], both[:, 128:256])
        if m == 1:
            down_send[...] = jnp.where(even, both[:, 128:256], both[:, 0:128])
            downs[core] = down
    down_copy = remote(down_send, downs.at[core], down_sem.at[0], down_sem.at[1], {"leaf": mate})


    arrive(3)

    def own_step(i, carry):
        acc[:, lanes(i)] = near_rows((3,), i)
        return carry

    lax.fori_loop(0, 8, own_step, 0, unroll=4)
    down_copy.wait_recv()
    descend(96, 128, jnp.concatenate([downs[0], downs[1]], axis=0))
    for c in sums:
        c.wait_recv()
    for h in range(2):

        def final_step(k, carry):
            i = 4 * h + k
            total = acc[:, lanes(i)] + far_rows(3, i)
            total = total + recv_buf[0, h, :, lanes(k)].astype(F32) + recv_buf[1, h, :, lanes(k)].astype(F32)
            out[:, lanes(i)] = total.astype(BF16)
            return carry

        lax.fori_loop(0, 4, final_step, 0, unroll=4)
    for c in sends:
        c.wait_send()


def local(
    vectors,
    near_blocks,
    near_cols,
    near_count,
    col_basis,
    row_basis,
    local_transfer,
    local_coupling,
    local_partners,
    upper_transfer,
    upper_coupling,
    upper_partners,
):
    anywhere = pl.BlockSpec(memory_space=pl.ANY)
    scalars = pl.BlockSpec(memory_space=pltpu.SMEM)
    dma = pltpu.SemaphoreType.DMA
    vm = pltpu.VMEM
    return pl.pallas_call(
        kernel,
        out_shape=jax.ShapeDtypeStruct((64, 2048), BF16),
        in_specs=[
            anywhere,
            anywhere,
            scalars,
            scalars,
            anywhere,
            anywhere,
            anywhere,
            anywhere,
            scalars,
            anywhere,
            anywhere,
            anywhere,
        ],
        out_specs=pl.BlockSpec(memory_space=pltpu.VMEM),
        scratch_shapes=[vm((24, 64, 256), BF16) for _ in range(4)]
        + [
            vm((8, 8, 256, 256), BF16),
            vm((64, 2048), BF16),
            vm((64, 2048), BF16),
            vm((8, 256, 256), BF16),
            vm((7, 64, 128), BF16),
            vm((15, 64, 128), BF16),
            vm((31, 64, 128), BF16),
            vm((64, 128), BF16),
            vm((4, 6, 64, 128), BF16),
            pltpu.SMEM((4, 2, 63), jnp.int32),
            vm((3, 15, 128, 128), BF16),
            vm((15, 128, 128), F32),
            vm((7, 128, 256), BF16),
            vm((31, 128, 256), BF16),
            vm((4, 8, 64, 256), BF16),
            vm((2, 16, 128), BF16),
            vm((4, 8, 16, 128), BF16),
            vm((31, 16, 128), BF16),
            vm((16, 128), F32),
            vm((2, 16, 128), F32),
            vm((2, 64, 1024), BF16),
            vm((2, 64, 1024), BF16),
            vm((2, 2, 64, 1024), BF16),
            vm((2, 2, 64, 1024), BF16),
            vm((64, 2048), F32),
            vm((64, 1024), F32),
            dma((11,)),
            dma((4, 8)),
            dma((8,)),
            dma((6,)),
            dma((4, 2)),
            dma((4, 2)),
            dma((3,)),
            dma((3,)),
            dma((3,)),
            dma((3,)),
            dma((3,)),
            dma((3,)),
            dma((2,)),
            dma((2,)),
            dma((2,)),
            dma((2,)),
            dma((2,)),
            dma((3,)),
            dma((3,)),
            dma((7,)),
            dma((7,)),
            dma((3, 2)),
            dma((3, 2)),
        ],
        compiler_params=pltpu.CompilerParams(
            collective_id=0, has_side_effects=True, vmem_limit_bytes=63 * 1024 * 1024
        ),
        name="h2",
    )(
        vectors,
        near_blocks,
        near_cols,
        near_count,
        col_basis,
        row_basis,
        local_transfer,
        local_coupling,
        local_partners.T,
        upper_transfer,
        upper_coupling,
        upper_partners.T,
    )


def solution(mesh):
    return jax.shard_map(
        local,
        mesh=mesh,
        in_specs=(
            P(None, "leaf"),
            P("leaf", "near", None, None),
            P("leaf", "near"),
            P("leaf"),
            P(None, "leaf"),
            P(None, "leaf"),
            P("leaf", None, None),
            P("leaf", None, "near"),
            P("leaf", "near"),
            P(),
            P(None, None, "near"),
            P(None, "near"),
        ),
        out_specs=P("near", "leaf"),
        check_vma=False,
    )
```
